128 devices in a mesh: dp: 8 (over z, y_hi), expert: 16 (over y_lo, x, core).
Axes of the slice: x: 4, y: 4 (y_hi: 2, y_lo: 2; y = y_hi * 2 + y_lo), z: 4, core: 2. Of those that a mesh axis runs over, the one named last changes fastest.
Arguments:
- tokens: bfloat16 [16384, 2048], P(('dp', 'expert')), may hold values from -6 to 6
- out_grad: bfloat16 [16384, 2048], P(('dp', 'expert')), may hold values from -1.5 to 1.5
- gate_probs: float32 [16384, 2], P(('dp', 'expert')), may hold values from 0.1 to 1
- expert_ids: int32 [16384, 2], P(('dp', 'expert')), may hold values from 0 to 31, all different within a row; in each aligned block of 128 rows (0 to 127, 128 to 255, ...) at most 12 rows name the same one
- gate_weight: bfloat16 [32, 2048, 2048], P('expert', None, 'dp'), may hold values from -0.125 to 0.125
- up_weight: bfloat16 [32, 2048, 2048], P('expert', None, 'dp'), may hold values from -0.125 to 0.125
- down_weight: bfloat16 [32, 2048, 2048], P('expert', 'dp'), may hold values from -0.125 to 0.125
Outputs:
- d_tokens: bfloat16 [16384, 2048], P(('dp', 'expert'))
- grad_gate: float32 [32, 2048, 2048], P('expert', None, 'dp')
- grad_up: float32 [32, 2048, 2048], P('expert', None, 'dp')
- grad_down: float32 [32, 2048, 2048], P('expert', 'dp')
The draws below stay inside these ranges and needn't reach their ends.
Inputs may be any that keep to these rules, and one draw needn't show every extreme that they name: `expert_ids`: each token names two different experts. Among the 128 tokens of one device no expert is named more than 12 times, a bound that some block reaches there.
All inputs are finite; a program needn't handle non-finite values.
Results may differ from the reference program's by a relative error of at most 0.014.
Values may be sent and summed in bfloat16 or wider, within the bound.
A program may use at most 192 MiB of HBM per device.

```python
import math
import jax
import jax.numpy as jnp
import numpy as np
from jax import lax

D = 2048
FF = 2048
TOK_DEV = 128
EXPERTS = 32
CAP = 12
TOKENS = 16384
N_DP = 8


def block_levels(rng, extent, cuts, low, top_value):
    level, own = 1.0, jax.random.fold_in(rng, 6)
    for axis_at, parts in cuts:
        steps = jnp.exp(jax.random.uniform(jax.random.fold_in(own, axis_at), (parts,), jnp.float32, low / len(cuts), top_value / len(cuts)))
        level = level * jnp.repeat(steps, extent[axis_at] // parts).reshape([-1 if axis == axis_at else 1 for axis in range(len(extent))])
    return level


def deal_out(own_key, own, number, rows, count, top, reach, slope):
    ranking = jax.random.permutation(own_key, count)
    heavy_load, common = load_shares(count, rows * top, reach, slope, True), load_shares(count, rows * top, reach, slope, False)
    places = jnp.arange(count)

    def named(lengths, turn):
        used = int((lengths > 0).sum())
        fixed = max(1, used // 4)
        shifted = fixed + (places - fixed + turn * (used - fixed)) % max(1, count - fixed)
        return jnp.zeros((count,), jnp.int32).at[ranking[jnp.where(places < fixed, places, shifted)]].set(jnp.asarray(lengths, jnp.int32))

    lengths = jnp.where(number % 4 == 0, named(heavy_load, number // 4), named(common, number - number // 4 - 1))
    mixed = jax.random.permutation(jax.random.fold_in(own, 3), count)
    giver, receiver = mixed[0:count // 2 * 2:2], mixed[1:count // 2 * 2:2]
    slack = jnp.minimum(lengths[giver] - 1, reach - lengths[receiver]) // 2
    slack = jnp.where((giver == ranking[0]) | (receiver == ranking[0]) | (lengths[receiver] == 0), 0, jnp.maximum(slack, 0))
    shifted = jax.random.randint(jax.random.fold_in(own, 4), (count // 2,), 0, 1 << 20) % (slack + 1)
    lengths = lengths.at[giver].add(-shifted).at[receiver].add(shifted)
    members = jnp.searchsorted(jnp.cumsum(lengths), jnp.arange(rows * top), side="right").astype(jnp.int32)
    table = members.reshape(top, rows).T
    table = table[jax.random.permutation(jax.random.fold_in(own, 1), rows)]
    turn = jax.random.randint(jax.random.fold_in(own, 2), (rows, 1), 0, top)
    return jnp.take_along_axis(table, (jnp.arange(top)[None, :] + turn) % top, axis=1)


def load_shares(count, total, most, lean, full):
    loads = [(1 << 20) // math.isqrt(grade ** lean) + 1 for grade in range(1, count + 1)]
    largest = most if full else min(most, max(-(-total // count), total * loads[0] // sum(loads)))
    least = 1 if total - largest >= count - 1 else 0
    holding, rest = [largest] + [least] * (count - 1), total - largest - least * (count - 1)
    while rest > 0:
        free = [i for i in range(1, count) if holding[i] < largest] or [i for i in range(1, count) if holding[i] < most]
        whole, left = sum([loads[i] for i in free]), rest
        for i in free:
            extra = min(most - holding[i], max(1, left * loads[i] // whole), rest)
            holding[i] = holding[i] + extra
            rest = rest - extra
    return np.array(holding)


def normal_values(rng, extent, width, most, shards=(), kind=jnp.bfloat16):
    array = width * jax.random.normal(rng, extent, jnp.float32)
    if shards:
        array = array * block_levels(rng, extent, shards, -0.22, 0.18)
    return jnp.clip(array, -most, most).astype(kind)


def setup_inputs(seed: int = 0) -> dict:
    keys = jax.random.split(jax.random.key(seed), 8)
    tokens = normal_values(keys[0], (TOKENS, D), 1.0, 6.0, ((0, 128),))
    out_grad = normal_values(keys[1], (TOKENS, D), 0.25, 1.5, ((0, 128),))
    gate_probs = jnp.clip(0.1 + 0.9 * jax.random.uniform(keys[2], (TOKENS, 2), jnp.float32) ** block_levels(keys[2], (TOKENS, 2), ((0, 128),), -0.2, 0.2), 0.1, 1.0)
    expert_ids_keys = jax.random.split(jax.random.fold_in(keys[3], 1), TOKENS // TOK_DEV)
    expert_ids_turns = jax.random.permutation(jax.random.fold_in(keys[3], 3), TOKENS // TOK_DEV)
    expert_ids = jax.vmap(lambda own, number: deal_out(jax.random.fold_in(keys[3], 2), own, number, TOK_DEV, EXPERTS, 2, CAP, 2))(expert_ids_keys, expert_ids_turns).reshape((TOKENS, 2))
    gate_weight = normal_values(keys[4], (EXPERTS, D, FF), D ** -0.5, 0.125, ((0, 16), (2, 8)))
    up_weight = normal_values(keys[5], (EXPERTS, D, FF), D ** -0.5, 0.125, ((0, 16), (2, 8)))
    down_weight = normal_values(keys[6], (EXPERTS, FF, D), FF ** -0.5, 0.125, ((0, 16), (1, 8)))
    return dict(tokens=tokens, out_grad=out_grad, gate_probs=gate_probs, expert_ids=expert_ids, gate_weight=gate_weight, up_weight=up_weight, down_weight=down_weight)


def expert_backward(inputs):
    rows_in, grads_in, w_gate, w_up, w_down = inputs
    gate_pre = jnp.dot(rows_in, w_gate, preferred_element_type=jnp.float32)
    up_pre = jnp.dot(rows_in, w_up, preferred_element_type=jnp.float32)
    gate_sigmoid = jax.nn.sigmoid(gate_pre)
    gate_silu = gate_pre * gate_sigmoid
    hidden_act = (gate_silu * up_pre).astype(jnp.bfloat16)
    hidden_grad = jnp.dot(grads_in, w_down.T, preferred_element_type=jnp.float32)
    grad_down = jnp.dot(hidden_act.T, grads_in, preferred_element_type=jnp.float32)
    gate_grad = (hidden_grad * up_pre * gate_sigmoid * (1.0 + gate_pre * (1.0 - gate_sigmoid))).astype(jnp.bfloat16)
    up_grad = (hidden_grad * gate_silu).astype(jnp.bfloat16)
    grad_gate = jnp.dot(rows_in.T, gate_grad, preferred_element_type=jnp.float32)
    grad_up = jnp.dot(rows_in.T, up_grad, preferred_element_type=jnp.float32)
    count = rows_in.shape[0]
    group_size = FF // N_DP
    gate_groups = gate_grad.astype(jnp.float32).reshape(count, N_DP, group_size)
    up_groups = up_grad.astype(jnp.float32).reshape(count, N_DP, group_size)
    wg_groups = w_gate.astype(jnp.float32).reshape(D, N_DP, group_size)
    wu_groups = w_up.astype(jnp.float32).reshape(D, N_DP, group_size)
    group_terms = jnp.einsum("rgh,dgh->rgd", gate_groups, wg_groups) + jnp.einsum("rgh,dgh->rgd", up_groups, wu_groups)
    rounded = lax.optimization_barrier(group_terms.astype(jnp.bfloat16))
    slot_grads = jnp.sum(rounded.astype(jnp.float32), axis=1).astype(jnp.bfloat16)
    return grad_gate, grad_up, grad_down, slot_grads


def reference(tokens, out_grad, gate_probs, expert_ids, gate_weight, up_weight, down_weight):
    devices = TOKENS // TOK_DEV
    block_ids = expert_ids.reshape(devices, 2 * TOK_DEV)
    onehot = (block_ids[:, :, None] == jnp.arange(EXPERTS, dtype=jnp.int32)[None, None, :]).astype(jnp.int32)
    earlier = jnp.cumsum(onehot, axis=1) - onehot
    slot = jnp.sum(earlier * onehot, axis=2)
    position = (jnp.arange(devices, dtype=jnp.int32)[:, None] * CAP + slot).reshape(-1).astype(jnp.int32)
    flat_ids = expert_ids.reshape(-1).astype(jnp.int32)
    token_rows = jnp.repeat(tokens, 2, axis=0)
    scaled = (gate_probs.reshape(-1, 1) * jnp.repeat(out_grad, 2, axis=0).astype(jnp.float32)).astype(jnp.bfloat16)
    expert_rows = jnp.zeros((EXPERTS, devices * CAP, D), jnp.bfloat16).at[flat_ids, position].set(token_rows)
    expert_grads = jnp.zeros((EXPERTS, devices * CAP, D), jnp.bfloat16).at[flat_ids, position].set(scaled)
    grad_gate, grad_up, grad_down, slot_grads = lax.map(expert_backward, (expert_rows, expert_grads, gate_weight, up_weight, down_weight))
    picked = slot_grads[flat_ids, position]
    d_tokens = jnp.sum(picked.reshape(TOKENS, 2, D).astype(jnp.float32), axis=1).astype(jnp.bfloat16)
    return d_tokens, grad_gate, grad_up, grad_down
```

```python
import jax
import jax.numpy as jnp
from jax import lax
from jax.sharding import Mesh, PartitionSpec as P

CAP = 12
PLANE = ("yh", "yl", "x", "c")
BF = jnp.bfloat16
F32 = jnp.float32


def dot(a, b, dims):
    return lax.dot_general(a, b, (dims, ((), ())), preferred_element_type=F32)


def route(ids):
    flat = ids.reshape(-1)
    n = flat.shape[0]
    onehot = (flat[:, None] == jnp.arange(32, dtype=jnp.int32)[None, :])
    row = lax.broadcasted_iota(jnp.int32, (n, n), 0)
    col = lax.broadcasted_iota(jnp.int32, (n, n), 1)
    earlier = dot((col < row).astype(BF), onehot.astype(BF), ((1,), (0,)))
    slot = jnp.sum(jnp.where(onehot, earlier, 0.0), axis=1)
    return slot.reshape(ids.shape)


def places(meta, j):
    ids, slot = meta[:, 0:2].astype(jnp.int32), meta[:, 2:4].astype(jnp.int32)
    return jnp.where(ids % 2 == j, (ids // 2) * CAP + slot, -1)


def dispatch(both, meta, j):
    place = places(meta, j)
    probs = meta[:, 4:6]
    r = lax.broadcasted_iota(jnp.int32, (384, 1), 0)
    column, rest = r // 24, r % 24
    is_grad = rest >= 12
    want = column * CAP + rest % CAP
    hit0 = want == place[:, 0][None, :]
    hit1 = want == place[:, 1][None, :]
    hit = (hit0 | hit1)
    pick = jnp.concatenate([hit & ~is_grad, hit & is_grad], axis=1).astype(BF)
    prob = jnp.sum(jnp.where(hit0, probs[:, 0][None, :], 0.0) + jnp.where(hit1, probs[:, 1][None, :], 0.0), axis=1, keepdims=True)
    scale = jnp.where(is_grad, prob, 1.0)
    return (dot(pick, both, ((1,), (0,))) * scale).astype(BF)


def forward(rows, wg, wu, wd):
    rows = rows.reshape(32, 2, CAP, -1)
    x = rows[:, 0].reshape(32 * CAP, -1)
    g = rows[:, 1].reshape(32 * CAP, -1)
    gate = dot(x, wg, ((1,), (0,)))
    up = dot(x, wu, ((1,), (0,)))
    hid = dot(g, wd, ((1,), (1,)))
    s = jax.nn.sigmoid(gate)
    silu = gate * s
    act = (silu * up).astype(BF)
    gg = (hid * up * s * (1.0 + gate * (1.0 - s))).astype(BF)
    ug = (hid * silu).astype(BF)
    part = (dot(gg, wg, ((1,), (1,))) + dot(ug, wu, ((1,), (1,)))).astype(BF)
    return part, (x, g, act, gg, ug)


def combine(back, meta):
    total = 0.0
    for j in range(2):
        place = places(meta, j)
        r = lax.broadcasted_iota(jnp.int32, (1, 384), 1) % 192
        pick = ((r == place[:, 0:1]) | (r == place[:, 1:2])).astype(BF)
        total = total + dot(pick, back[j].reshape(384, -1), ((1,), (0,)))
    return total


def body(tokens, out_grad, probs, ids, wg, wu, wd):
    up1 = [(i, (i + 1) % 4) for i in range(4)]
    dn1 = [(i, (i + 3) % 4) for i in range(4)]
    far = [(i, (i + 2) % 4) for i in range(4)]
    both = jnp.concatenate([tokens, out_grad], axis=0)
    meta = jnp.concatenate([ids.astype(F32), route(ids), probs, jnp.zeros_like(probs)], axis=1)
    both_o = lax.ppermute(both, "z", far)
    meta_o = lax.ppermute(meta, "z", far)

    def spread(b, m, j):
        send = dispatch(b, m, j)
        send = jnp.concatenate([send, send], axis=0)
        return lax.all_to_all(send, PLANE, split_axis=0, concat_axis=0, tiled=True)

    def gather_back(part):
        return lax.all_to_all(part.reshape(32 * 24, -1), PLANE, split_axis=0, concat_axis=0, tiled=True)

    near, above, below, opp = [], [], [], []
    for j in range(2):
        near.append(spread(both, meta, j))
        below.append(lax.ppermute(near[j], "z", up1))
        above.append(lax.ppermute(near[j], "z", dn1))
    for j in range(2):
        opp.append(spread(both_o, meta_o, j))
    kept = [[], []]
    sums, sums_o = [], []
    for j in range(2):
        w = (wg[j], wu[j], wd[j])
        p_near, k = forward(near[j], *w)
        kept[j].append(k)
        p_opp, k = forward(opp[j], *w)
        kept[j].append(k)
        p_below, k = forward(below[j], *w)
        kept[j].append(k)
        p_above, k = forward(above[j], *w)
        kept[j].append(k)
        p_below = lax.ppermute(p_below, "z", dn1)
        p_above = lax.ppermute(p_above, "z", up1)
        sums.append((p_near.astype(F32) + p_below.astype(F32) + p_above.astype(F32)).astype(BF).reshape(32, CAP, -1))
        sums_o.append(p_opp.reshape(32, CAP, -1))
    back_o = gather_back(jnp.concatenate(sums_o, axis=1)).reshape(32, 2, CAP, -1)
    part_o = combine([back_o[:, 0], back_o[:, 1]], meta_o).astype(BF)
    part_o = lax.ppermute(part_o, "z", far)
    back = gather_back(jnp.concatenate(sums, axis=1)).reshape(32, 2, CAP, -1)
    d_tokens = (combine([back[:, 0], back[:, 1]], meta) + part_o.astype(F32)).astype(BF)
    gw, gu, gd = [], [], []
    for j in range(2):
        gw.append(sum(dot(x, gg, ((0,), (0,))) for x, g, act, gg, ug in kept[j]))
        gu.append(sum(dot(x, ug, ((0,), (0,))) for x, g, act, gg, ug in kept[j]))
        gd.append(sum(dot(act, g, ((0,), (0,))) for x, g, act, gg, ug in kept[j]))
    return d_tokens, jnp.stack(gw), jnp.stack(gu), jnp.stack(gd)


def solution(mesh):
    fine = Mesh(mesh.devices.reshape(4, 2, 2, 4, 2), ("z", "yh", "yl", "x", "c"))
    dp, expert = ("z", "yh"), ("yl", "x", "c")
    tok = P(dp + expert, None)
    return jax.shard_map(
        body,
        mesh=fine,
        in_specs=(tok, tok, tok, tok, P(expert, None, dp), P(expert, None, dp), P(expert, dp, None)),
        out_specs=(tok, P(expert, None, dp), P(expert, None, dp), P(expert, dp, None)),
        check_vma=False,
    )
```

```python
import jax
import jax.numpy as jnp
from jax import lax
from jax.experimental import pallas as pl
from jax.experimental.pallas import tpu as pltpu
from jax.sharding import PartitionSpec as P

MESH = pl.DeviceIdType.MESH
BF = jnp.bfloat16
F32 = jnp.float32
CAP = 12
MSG = 4 * CAP
BLK = 4 * MSG
HALF = 4 * BLK
ROWS = 8 * BLK
WIDE = 512
AT = ((1,), (0,))
TB = ((1,), (1,))
TA = ((0,), (0,))


def dot(a, b, dims):
    return lax.dot_general(a, b, (dims, ((), ())), preferred_element_type=F32)


def place():
    dp, ex = lax.axis_index("dp"), lax.axis_index("expert")
    return lax.rem(lax.div(ex, 2), 4), lax.rem(dp, 2) * 2 + lax.div(ex, 8), lax.div(dp, 2), lax.rem(ex, 2)


def device(x, y, z, c):
    return (z * 2 + lax.div(y, 2), lax.rem(y, 2) * 8 + x * 2 + c)


def kernel(
    tokens, out_grad, meta_in, wg_hbm, wu_hbm, wd_hbm,
    d_out, gg_out, gu_out, gd_out, near, above, below, opp, ret_a, ret_b, back, back_o,
    both, far, meta, far_meta, msg, msg_o, perm, stage, tok, grad, hid, part, p_near, p_above, p_below, p_opp,
    rstage, dacc, dsend, dfar, wg, wu, wd, ag, au, ad,
    far_s, far_r, loc, near_s, near_r, opp_s, opp_r, fwd_s, above_r, below_r, pa_s, ret_s, reta_r, retb_r,
    back_s, back_r, backo_s, backo_r, dfar_s, dfar_r, st_s, out_s,
):
    x, y, z, c = place()
    up = device(x, y, lax.rem(z + 1, 4), c)
    down = device(x, y, lax.rem(z + 3, 4), c)
    over = device(x, y, lax.rem(z + 2, 4), c)

    def peer(k, dx, sign):
        dy, dc = lax.div(k, 2), lax.rem(k, 2)
        return device(lax.rem(x + sign * dx + 4, 4), lax.rem(y + sign * dy + 4, 4), z, lax.rem(c + dc, 2))

    loads = [
        pltpu.make_async_copy(tokens, both.at[pl.ds(0, 128)], loc.at[0]),
        pltpu.make_async_copy(out_grad, both.at[pl.ds(128, 128)], loc.at[1]),
        pltpu.make_async_copy(wg_hbm, wg, loc.at[2]),
        pltpu.make_async_copy(wu_hbm, wu, loc.at[3]),
        pltpu.make_async_copy(wd_hbm, wd, loc.at[4]),
    ]
    for cp in loads:
        cp.start()

    barrier = pltpu.get_barrier_semaphore()
    for other in (up, down, over):
        pl.semaphore_signal(barrier, inc=1, device_id=other, device_id_type=MESH)

    def greet(s, _):
        pl.semaphore_signal(barrier, inc=1, device_id=peer(lax.div(s, 4), lax.rem(s, 4), 1), device_id_type=MESH)
        return 0

    lax.fori_loop(1, 32, greet, 0)

    e0, e1 = meta_in[0:1, :], meta_in[1:2, :]
    ei = lax.broadcasted_iota(jnp.int32, (32, 128), 0).astype(F32)
    h0, h1 = ei == e0, ei == e1
    before = (lax.broadcasted_iota(jnp.int32, (128, 128), 0) < lax.broadcasted_iota(jnp.int32, (128, 128), 1))
    counts = jnp.where(h0 | h1, 1.0, 0.0).astype(BF)
    earlier = dot(counts, jnp.where(before, 1.0, 0.0).astype(BF), AT)

    def row_of(hit, e):
        slot = jnp.sum(jnp.where(hit, earlier, 0.0), axis=0, keepdims=True)
        return 24.0 * e - 12.0 * (e - 2.0 * jnp.floor(e * 0.5)) + slot

    meta[0:1, :] = row_of(h0, e0)
    meta[1:2, :] = row_of(h1, e1)
    meta[2:4, :] = meta_in[2:4, :]
    meta[4:8, :] = meta_in[4:8, :]

    ri = lax.broadcasted_iota(jnp.int32, (BLK, BLK), 0)
    ci = lax.broadcasted_iota(jnp.int32, (BLK, BLK), 1)
    src = lax.div(lax.rem(ri, MSG), CAP) * MSG + lax.div(ri, MSG) * CAP + lax.rem(ri, CAP)
    perm[...] = jnp.where(ci == src, 1.0, 0.0).astype(BF)

    pl.semaphore_wait(barrier, 34)
    fars = [
        pltpu.make_async_remote_copy(tokens, far.at[pl.ds(0, 128)], far_s.at[0], far_r.at[0], device_id=over, device_id_type=MESH),
        pltpu.make_async_remote_copy(out_grad, far.at[pl.ds(128, 128)], far_s.at[1], far_r.at[1], device_id=over, device_id_type=MESH),
        pltpu.make_async_remote_copy(meta, far_meta, far_s.at[2], far_r.at[2], device_id=over, device_id_type=MESH),
    ]
    for cp in fars:
        cp.start()

    def rows_of(k):
        dy, dc = lax.div(k, 2), lax.rem(k, 2)
        r = lax.broadcasted_iota(jnp.int32, (BLK, 1), 0)
        q = lax.rem(r, MSG)
        column = lax.rem(y + dy, 2) * 8 + lax.rem(x + lax.div(r, MSG), 4) * 2 + lax.rem(c + dc, 2)
        return (column * MSG + q).astype(F32), q

    def build(rows, m, out, g):
        want, q = rows_of(g)
        t0, t1, p0, p1 = m[0:1, :], m[1:2, :], m[2:3, :], m[3:4, :]
        hit_t = (want == t0) | (want == t1)
        hit0, hit1 = want - 24.0 == t0, want - 24.0 == t1
        hit_t = jnp.where(q < 24, jnp.where(hit_t, 1.0, 0.0), 0.0)
        hit0 = jnp.where(q >= 24, jnp.where(hit0, 1.0, 0.0), 0.0)
        hit1 = jnp.where(q >= 24, jnp.where(hit1, 1.0, 0.0), 0.0)
        pick = jnp.concatenate([hit_t, hit0 + hit1], axis=1).astype(BF)
        scale = jnp.sum(hit0 * p0 + hit1 * p1, axis=1, keepdims=True) + jnp.where(q < 24, 1.0, 0.0)
        base = pl.multiple_of(g * BLK, BLK)

        def part_of(n, _):
            cols = pl.ds(pl.multiple_of(n * WIDE, WIDE), WIDE)
            out[pl.ds(base, BLK), cols] = (dot(pick, rows[:, cols], AT) * scale).astype(BF)
            return 0

        lax.fori_loop(0, 2048 // WIDE, part_of, 0)

    def send_block(k, src_buf, dst_buf, ssem, rsem, base, sign, width):
        for dx in range(4):
            frm = src_buf.at[pl.ds(pl.multiple_of(base + dx * MSG, MSG), MSG), pl.ds(0, width)]
            to = dst_buf.at[pl.ds(pl.multiple_of(k * BLK + dx * MSG, MSG), MSG), pl.ds(0, width)]
            if dx == 0:
                @pl.when(k == 0)
                def _():
                    pltpu.make_async_copy(frm, to, rsem.at[k]).start()

                @pl.when(k > 0)
                def _():
                    pltpu.make_async_remote_copy(frm, to, ssem.at[0], rsem.at[k], device_id=peer(k, dx, sign), device_id_type=MESH).start()
            else:
                pltpu.make_async_remote_copy(frm, to, ssem.at[0], rsem.at[k], device_id=peer(k, dx, sign), device_id_type=MESH).start()

    def block(ref, k):
        return ref.at[pl.ds(pl.multiple_of(k * BLK, BLK), BLK)]

    def got(ref, k, sem):
        pltpu.make_async_copy(block(ref, k), block(ref, k), sem.at[k]).wait()

    loads[0].wait()
    loads[1].wait()

    def dispatch(rows, m, out, dst, ssem, rsem):
        def one(g, _):
            build(rows, m, out, g)
            base = g * BLK
            send_block(g, out, dst, ssem, rsem, base, 1, 2048)
            send_block(g + 4, out, dst, ssem, rsem, base, 1, 2048)
            return 0

        lax.fori_loop(0, 4, one, 0)

    dispatch(both, meta, msg, near, near_s, near_r)

    def clear(n, _):
        rows = pl.ds(pl.multiple_of(n * 256, 256), 256)
        for e in range(2):
            ag[e, rows, :] = jnp.zeros((256, 256), F32)
            au[e, rows, :] = jnp.zeros((256, 256), F32)
        return 0

    lax.fori_loop(0, 8, clear, 0)

    def clear_d(n, _):
        cols = pl.ds(pl.multiple_of(n * 256, 256), 256)
        for e in range(2):
            ad[e, :, cols] = jnp.zeros((256, 256), F32)
        return 0

    lax.fori_loop(0, 8, clear_d, 0)
    for cp in loads[2:]:
        cp.wait()

    def forward(k, _):
        got(near, k, near_r)
        pltpu.make_async_remote_copy(block(near, k), block(below, k), fwd_s.at[0], below_r.at[k], device_id=up, device_id_type=MESH).start()
        pltpu.make_async_remote_copy(block(near, k), block(above, k), fwd_s.at[1], above_r.at[k], device_id=down, device_id_type=MESH).start()
        return 0

    def half(ref, h):
        return ref.at[pl.ds(h * HALF, HALF)]

    def load(buf, h):
        return pltpu.make_async_copy(half(buf, h), stage, st_s.at[0])

    def compute(buf, h, out):
        cp = load(buf, h)
        cp.start()
        cp.wait()

        def sort_in(i, _):
            b, n = lax.div(i, 4), lax.rem(i, 4)
            cols = pl.ds(pl.multiple_of(n * WIDE, WIDE), WIDE)
            v = dot(perm[...], stage[pl.ds(pl.multiple_of(b * BLK, BLK), BLK), cols], AT).astype(BF)
            rows = pl.ds(pl.multiple_of(b * MSG, MSG), MSG)
            tok[0, rows, cols] = v[0:48]
            tok[1, rows, cols] = v[48:96]
            grad[0, rows, cols] = v[96:144]
            grad[1, rows, cols] = v[144:192]
            return 0

        lax.fori_loop(0, 16, sort_in, 0)

        def expert(e, _):
            gate = dot(tok[e], wg[e], AT)
            upv = dot(tok[e], wu[e], AT)
            hg = dot(grad[e], wd[e], TB)
            s = jax.nn.sigmoid(gate)
            silu = gate * s
            hid[0] = (silu * upv).astype(BF)
            hid[1] = (hg * upv * s * (1.0 + gate * (1.0 - s))).astype(BF)
            hid[2] = (hg * silu).astype(BF)

            def tile(n, _):
                cols = pl.ds(pl.multiple_of(n * WIDE, WIDE), WIDE)
                part[e, :, cols] = (dot(hid[1], wg[e, cols, :], TB) + dot(hid[2], wu[e, cols, :], TB)).astype(BF)
                ag[e, cols, :] += dot(tok[e, :, cols], hid[1], TA)
                au[e, cols, :] += dot(tok[e, :, cols], hid[2], TA)
                ad[e, :, cols] += dot(hid[0], grad[e, :, cols], TA)
                return 0

            lax.fori_loop(0, 2048 // WIDE, tile, 0)
            return 0

        lax.fori_loop(0, 2, expert, 0)

        def sort_out(i, _):
            b, n = lax.div(i, 2), lax.rem(i, 2)
            rows = pl.ds(pl.multiple_of(b * MSG, MSG), MSG)
            lo = pl.ds(pl.multiple_of(n * WIDE, WIDE), WIDE)
            hi = pl.ds(pl.multiple_of(n * WIDE + 1024, WIDE), WIDE)
            v = jnp.concatenate([part[0, rows, lo], part[1, rows, lo], part[0, rows, hi], part[1, rows, hi]], axis=0)
            out[pl.ds(pl.multiple_of(h * HALF + b * BLK, BLK), BLK), lo] = dot(perm[...], v, AT).astype(BF)
            return 0

        lax.fori_loop(0, 8, sort_out, 0)

    def got_half(ref, h, sem):
        def one(k, _):
            got(ref, k, sem)
            return 0

        lax.fori_loop(4 * h, 4 * h + 4, one, 0)

    def give(h):
        def one(k, _):
            pltpu.make_async_remote_copy(block(p_below, k), block(ret_a, k), ret_s.at[0], reta_r.at[k], device_id=down, device_id_type=MESH).start()
            pltpu.make_async_remote_copy(block(p_above, k), block(ret_b, k), ret_s.at[1], retb_r.at[k], device_id=up, device_id_type=MESH).start()
            return 0

        lax.fori_loop(4 * h, 4 * h + 4, one, 0)

    def settle(h):
        def one(k, _):
            got(ret_a, k, reta_r)
            got(ret_b, k, retb_r)
            ca = pltpu.make_async_copy(block(ret_a, k), rstage.at[pl.ds(0, BLK)], st_s.at[1])
            cb = pltpu.make_async_copy(block(ret_b, k), rstage.at[pl.ds(BLK, BLK)], st_s.at[2])
            ca.start()
            cb.start()
            ca.wait()
            cb.wait()
            rows = pl.ds(pl.multiple_of(k * BLK, BLK), BLK)
            p_near[rows, :] = (p_near[rows, :].astype(F32) + rstage[0:BLK, :].astype(F32) + rstage[BLK : 2 * BLK, :].astype(F32)).astype(BF)
            send_block(k, p_near, back, back_s, back_r, k * BLK, -1, 1024)
            return 0

        lax.fori_loop(4 * h, 4 * h + 4, one, 0)

    def combine(buf, sem, m):
        dacc[...] = jnp.zeros_like(dacc)

        def one(k, _):
            got(buf, k, sem)
            cp = pltpu.make_async_copy(block(buf, k), rstage.at[pl.ds(0, BLK)], st_s.at[1])
            cp.start()
            want, q = rows_of(k)
            t0, t1 = m[0:1, :], m[1:2, :]
            lo = jnp.where(q < 24, jnp.where((want == t0) | (want == t1), 1.0, 0.0), 0.0).astype(BF)
            hi = jnp.where(q >= 24, jnp.where((want - 24.0 == t0) | (want - 24.0 == t1), 1.0, 0.0), 0.0).astype(BF)
            cp.wait()
            dacc[:, 0:1024] += dot(lo, rstage[0:BLK, :], TA)
            dacc[:, 1024:2048] += dot(hi, rstage[0:BLK, :], TA)
            return 0

        lax.fori_loop(0, 8, one, 0)

    lax.fori_loop(0, 4, forward, 0)
    compute(near, 0, p_near)
    lax.fori_loop(4, 8, forward, 0)
    for cp in fars:
        cp.wait()
    dispatch(far, far_meta, msg_o, opp, opp_s, opp_r)
    compute(near, 1, p_near)

    got_half(below, 0, below_r)
    compute(below, 0, p_below)
    got_half(above, 0, above_r)
    compute(above, 0, p_above)
    give(0)

    def send_opp(k, _):
        send_block(k, p_opp, back_o, backo_s, backo_r, k * BLK, -1, 1024)
        return 0

    for h in range(2):
        got_half(opp, h, opp_r)
        compute(opp, h, p_opp)
        lax.fori_loop(4 * h, 4 * h + 4, send_opp, 0)

    got_half(below, 1, below_r)
    compute(below, 1, p_below)
    got_half(above, 1, above_r)
    compute(above, 1, p_above)
    give(1)

    outs = [
        pltpu.make_async_copy(ag, gg_out, out_s.at[0]),
        pltpu.make_async_copy(au, gu_out, out_s.at[1]),
        pltpu.make_async_copy(ad, gd_out, out_s.at[2]),
    ]
    for cp in outs:
        cp.start()

    settle(0)
    combine(back_o, backo_r, far_meta)
    dsend[...] = dacc[...].astype(BF)
    home = pltpu.make_async_remote_copy(dsend, dfar, dfar_s.at[0], dfar_r.at[0], device_id=over, device_id_type=MESH)
    home.start()
    settle(1)
    combine(back, back_r, meta)
    home.wait()
    dacc[...] = dacc[...] + dfar[...].astype(F32)
    dsend[...] = dacc[...].astype(BF)
    last = pltpu.make_async_copy(dsend, d_out, out_s.at[3])
    last.start()

    def sent(ref, rows, sem, i):
        pltpu.make_async_copy(ref.at[pl.ds(0, rows)], ref.at[pl.ds(0, rows)], sem.at[i]).wait()

    sent(near, 31 * MSG, near_s, 0)
    sent(opp, 31 * MSG, opp_s, 0)
    sent(near, ROWS, fwd_s, 0)
    sent(near, ROWS, fwd_s, 1)
    sent(ret_a, ROWS, ret_s, 0)
    sent(ret_b, ROWS, ret_s, 1)
    sent(back, 31 * MSG, back_s, 0)
    sent(back_o, 31 * MSG, backo_s, 0)
    for cp in outs:
        cp.wait()
    last.wait()


def body(tokens, out_grad, probs, ids, wg, wu, wd):
    meta = jnp.concatenate([ids.T.astype(F32), probs.T, jnp.zeros((4, 128), F32)], axis=0)
    hbm = pl.BlockSpec(memory_space=pltpu.HBM)
    vm = pl.BlockSpec(memory_space=pltpu.VMEM)
    sd = jax.ShapeDtypeStruct
    wide, slim = sd((ROWS, 2048), BF), sd((ROWS, 1024), BF)
    dma = pltpu.SemaphoreType.DMA
    outs = pl.pallas_call(
        kernel,
        name="expert_backward",
        out_shape=[
            sd((128, 2048), BF), sd((2, 2048, 256), F32), sd((2, 2048, 256), F32), sd((2, 256, 2048), F32),
            wide, wide, wide, wide, slim, slim, slim, slim,
        ],
        in_specs=[hbm, hbm, vm, hbm, hbm, hbm],
        out_specs=[hbm] * 12,
        scratch_shapes=[
            pltpu.VMEM((256, 2048), BF), pltpu.VMEM((256, 2048), BF), pltpu.VMEM((8, 128), F32), pltpu.VMEM((8, 128), F32),
            pltpu.VMEM((4 * BLK, 2048), BF), pltpu.VMEM((4 * BLK, 2048), BF), pltpu.VMEM((BLK, BLK), BF),
            pltpu.VMEM((HALF, 2048), BF), pltpu.VMEM((2, BLK, 2048), BF), pltpu.VMEM((2, BLK, 2048), BF),
            pltpu.VMEM((3, BLK, 256), BF), pltpu.VMEM((2, BLK, 2048), BF),
            pltpu.VMEM((ROWS, 1024), BF), pltpu.VMEM((ROWS, 1024), BF), pltpu.VMEM((ROWS, 1024), BF), pltpu.VMEM((ROWS, 1024), BF),
            pltpu.VMEM((2 * BLK, 1024), BF), pltpu.VMEM((128, 2048), F32), pltpu.VMEM((128, 2048), BF), pltpu.VMEM((128, 2048), BF),
            pltpu.VMEM((2, 2048, 256), BF), pltpu.VMEM((2, 2048, 256), BF), pltpu.VMEM((2, 256, 2048), BF),
            pltpu.VMEM((2, 2048, 256), F32), pltpu.VMEM((2, 2048, 256), F32), pltpu.VMEM((2, 256, 2048), F32),
            dma((3,)), dma((3,)), dma((5,)), dma((1,)), dma((8,)), dma((1,)), dma((8,)), dma((2,)), dma((8,)), dma((8,)),
            dma((1,)), dma((2,)), dma((8,)), dma((8,)), dma((1,)), dma((8,)), dma((1,)), dma((8,)), dma((1,)), dma((1,)),
            dma((3,)), dma((4,)),
        ],
        compiler_params=pltpu.CompilerParams(collective_id=0, has_side_effects=True, vmem_limit_bytes=62 * 2**20),
    )(tokens, out_grad, meta, wg, wu, wd)
    return tuple(outs[:4])


def solution(mesh):
    tok = P(("dp", "expert"), None)
    col, row = P("expert", None, "dp"), P("expert", "dp", None)
    return jax.shard_map(
        body, mesh=mesh, in_specs=(tok, tok, tok, tok, col, col, row), out_specs=(tok, col, col, row), check_vma=False
    )
```

```python
import functools

import jax
import jax.numpy as jnp
from jax import lax
from jax.experimental import pallas as pl
from jax.experimental.pallas import tpu as pltpu
from jax.sharding import PartitionSpec as P

MESH = pl.DeviceIdType.MESH
BF = jnp.bfloat16
F32 = jnp.float32
CAP = 12
MSG = 4 * CAP
BLK = 4 * MSG
HALF = 4 * BLK
ROWS = 8 * BLK
WIDE = 512
AT = ((1,), (0,))
TB = ((1,), (1,))
TA = ((0,), (0,))


def dot(a, b, dims):
    return lax.dot_general(a, b, (dims, ((), ())), preferred_element_type=F32)


def place():
    dp, ex = lax.axis_index("dp"), lax.axis_index("expert")
    return lax.rem(lax.div(ex, 2), 4), lax.rem(dp, 2) * 2 + lax.div(ex, 8), lax.div(dp, 2), lax.rem(ex, 2)


def device(x, y, z, c):
    return (z * 2 + lax.div(y, 2), lax.rem(y, 2) * 8 + x * 2 + c)


def kernel(
    tokens, out_grad, meta_in, wg_hbm, wu_hbm, wd_hbm,
    d_out, gg_out, gu_out, gd_out, near, above, below, opp, ret_a, ret_b, back, back_o,
    both, far, meta, far_meta, msg, msg_o, perm, stage, tok, grad, act, hid, part, p_near, p_above, p_below, p_opp,
    rstage, dacc, dsend, dfar, wgu, wd, agu, ad, dout,
    far_s, far_r, loc, near_s, near_r, opp_s, opp_r, fwd_s, above_r, below_r, pa_s, ret_s, reta_r, retb_r,
    back_s, back_r, backo_s, backo_r, dfar_s, dfar_r, st_s, out_s, stage_s,
):
    x, y, z, c = place()
    up = device(x, y, lax.rem(z + 1, 4), c)
    down = device(x, y, lax.rem(z + 3, 4), c)
    over = device(x, y, lax.rem(z + 2, 4), c)

    def peer(k, dx, sign):
        dy, dc = lax.rem(lax.div(k, 2) + dx, 4), lax.rem(k, 2)
        return device(lax.rem(x + sign * dx + 4, 4), lax.rem(y + sign * dy + 4, 4), z, lax.rem(c + dc, 2))

    loads = [
        pltpu.make_async_copy(tokens, both.at[pl.ds(0, 128)], loc.at[0]),
        pltpu.make_async_copy(out_grad, both.at[pl.ds(128, 128)], loc.at[1]),
        pltpu.make_async_copy(wg_hbm, wgu.at[:, :, pl.ds(0, 256)], loc.at[2]),
        pltpu.make_async_copy(wu_hbm, wgu.at[:, :, pl.ds(256, 256)], loc.at[3]),
        pltpu.make_async_copy(wd_hbm, wd, loc.at[4]),
    ]
    for cp in loads:
        cp.start()

    barrier = pltpu.get_barrier_semaphore()
    for other in (up, down, over):
        pl.semaphore_signal(barrier, inc=1, device_id=other, device_id_type=MESH)

    def greet(s, _):
        pl.semaphore_signal(barrier, inc=1, device_id=peer(lax.div(s, 4), lax.rem(s, 4), 1), device_id_type=MESH)
        return 0

    lax.fori_loop(1, 32, greet, 0)

    e0, e1 = meta_in[0:1, :], meta_in[1:2, :]
    ei = lax.broadcasted_iota(jnp.int32, (32, 128), 0).astype(F32)
    h0, h1 = ei == e0, ei == e1
    before = (lax.broadcasted_iota(jnp.int32, (128, 128), 0) < lax.broadcasted_iota(jnp.int32, (128, 128), 1))
    counts = jnp.where(h0 | h1, 1.0, 0.0).astype(BF)
    earlier = dot(counts, jnp.where(before, 1.0, 0.0).astype(BF), AT)

    def row_of(hit, e):
        slot = jnp.sum(jnp.where(hit, earlier, 0.0), axis=0, keepdims=True)
        return 24.0 * e - 12.0 * (e - 2.0 * jnp.floor(e * 0.5)) + slot

    meta[0:1, :] = row_of(h0, e0)
    meta[1:2, :] = row_of(h1, e1)
    meta[2:4, :] = meta_in[2:4, :]
    meta[4:8, :] = meta_in[4:8, :]

    ri = lax.broadcasted_iota(jnp.int32, (BLK, BLK), 0)
    ci = lax.broadcasted_iota(jnp.int32, (BLK, BLK), 1)
    src = lax.div(lax.rem(ri, MSG), CAP) * MSG + lax.div(ri, MSG) * CAP + lax.rem(ri, CAP)
    perm[...] = jnp.where(ci == src, 1.0, 0.0).astype(BF)

    pl.semaphore_wait(barrier, 34)
    fars = [
        pltpu.make_async_remote_copy(tokens, far.at[pl.ds(0, 128)], far_s.at[0], far_r.at[0], device_id=over, device_id_type=MESH),
        pltpu.make_async_remote_copy(out_grad, far.at[pl.ds(128, 128)], far_s.at[1], far_r.at[1], device_id=over, device_id_type=MESH),
        pltpu.make_async_remote_copy(meta, far_meta, far_s.at[2], far_r.at[2], device_id=over, device_id_type=MESH),
    ]
    for cp in fars:
        cp.start()

    def rows_of(k):
        r = lax.broadcasted_iota(jnp.int32, (BLK, 1), 0)
        q, dx = lax.rem(r, MSG), lax.div(r, MSG)
        column = lax.rem(y + lax.div(k, 2) + dx, 2) * 8 + lax.rem(x + dx, 4) * 2 + lax.rem(c + lax.rem(k, 2), 2)
        return (column * MSG + q).astype(F32), q

    def build(rows, m, out, g):
        want, q = rows_of(g)
        t0, t1, p0, p1 = m[0:1, :], m[1:2, :], m[2:3, :], m[3:4, :]
        hit_t = (want == t0) | (want == t1)
        hit0, hit1 = want - 24.0 == t0, want - 24.0 == t1
        hit_t = jnp.where(q < 24, jnp.where(hit_t, 1.0, 0.0), 0.0)
        hit0 = jnp.where(q >= 24, jnp.where(hit0, 1.0, 0.0), 0.0)
        hit1 = jnp.where(q >= 24, jnp.where(hit1, 1.0, 0.0), 0.0)
        pick = jnp.concatenate([hit_t, hit0 + hit1], axis=1).astype(BF)
        scale = jnp.sum(hit0 * p0 + hit1 * p1, axis=1, keepdims=True) + jnp.where(q < 24, 1.0, 0.0)
        base = pl.multiple_of(g * BLK, BLK)

        def part_of(n, _):
            cols = pl.ds(pl.multiple_of(n * WIDE, WIDE), WIDE)
            out[pl.ds(base, BLK), cols] = (dot(pick, rows[:, cols], AT) * scale).astype(BF)
            return 0

        lax.fori_loop(0, 2048 // WIDE, part_of, 0)

    def send_block(k, src_buf, dst_buf, ssem, rsem, base, sign, width):
        for dx in range(4):
            frm = src_buf.at[pl.ds(pl.multiple_of(base + dx * MSG, MSG), MSG), pl.ds(0, width)]
            to = dst_buf.at[pl.ds(pl.multiple_of(k * BLK + dx * MSG, MSG), MSG), pl.ds(0, width)]
            if dx == 0:
                @pl.when(k == 0)
                def _():
                    pltpu.make_async_copy(frm, to, rsem.at[k]).start()

                @pl.when(k > 0)
                def _():
                    pltpu.make_async_remote_copy(frm, to, ssem.at[0], rsem.at[k], device_id=peer(k, dx, sign), device_id_type=MESH).start()
            else:
                pltpu.make_async_remote_copy(frm, to, ssem.at[0], rsem.at[k], device_id=peer(k, dx, sign), device_id_type=MESH).start()

    def block(ref, k):
        return ref.at[pl.ds(pl.multiple_of(k * BLK, BLK), BLK)]

    def got(ref, k, sem):
        pltpu.make_async_copy(block(ref, k), block(ref, k), sem.at[k]).wait()

    loads[0].wait()
    loads[1].wait()

    def dispatch(rows, m, out, dst, ssem, rsem):
        def one(g, _):
            build(rows, m, out, g)
            base = g * BLK
            send_block(g, out, dst, ssem, rsem, base, 1, 2048)
            return 0

        def again(g, _):
            send_block(g + 4, out, dst, ssem, rsem, g * BLK, 1, 2048)
            return 0

        lax.fori_loop(0, 4, one, 0)
        lax.fori_loop(0, 4, again, 0)

    dispatch(both, meta, msg, near, near_s, near_r)

    def clear(n, _):
        rows = pl.ds(pl.multiple_of(n * 256, 256), 256)
        for e in range(2):
            agu[e, rows, :] = jnp.zeros((256, 512), F32)
        return 0

    lax.fori_loop(0, 8, clear, 0)

    def clear_d(n, _):
        cols = pl.ds(pl.multiple_of(n * 256, 256), 256)
        for e in range(2):
            ad[e, :, cols] = jnp.zeros((256, 256), F32)
        return 0

    lax.fori_loop(0, 8, clear_d, 0)
    for cp in loads[2:]:
        cp.wait()

    def forward(k, _):
        got(near, k, near_r)
        pltpu.make_async_remote_copy(block(near, k), block(below, k), fwd_s.at[0], below_r.at[k], device_id=up, device_id_type=MESH).start()
        pltpu.make_async_remote_copy(block(near, k), block(above, k), fwd_s.at[1], above_r.at[k], device_id=down, device_id_type=MESH).start()
        return 0

    def load(buf, h, b):
        return pltpu.make_async_copy(
            buf.at[pl.ds(pl.multiple_of(h * HALF + b * BLK, BLK), BLK)], stage.at[pl.ds(pl.multiple_of(b * BLK, BLK), BLK)], stage_s.at[b]
        )

    def compute(buf, h, out):
        for b in range(4):
            load(buf, h, b).start()

        def sort_in(i, _):
            b, n = lax.div(i, 4), lax.rem(i, 4)

            @pl.when(n == 0)
            def _():
                load(buf, h, b).wait()

            cols = pl.ds(pl.multiple_of(n * WIDE, WIDE), WIDE)
            v = dot(perm[...], stage[pl.ds(pl.multiple_of(b * BLK, BLK), BLK), cols], AT).astype(BF)
            rows = pl.ds(pl.multiple_of(b * MSG, MSG), MSG)
            tok[0, rows, cols] = v[0:48]
            tok[1, rows, cols] = v[48:96]
            grad[0, rows, cols] = v[96:144]
            grad[1, rows, cols] = v[144:192]
            return 0

        lax.fori_loop(0, 16, sort_in, 0)

        def expert(e, _):
            gate = dot(tok[e], wgu[e, :, 0:256], AT)
            upv = dot(tok[e], wgu[e, :, 256:512], AT)
            hg = dot(grad[e], wd[e], TB)
            s = jax.nn.sigmoid(gate)
            silu = gate * s
            act[...] = (silu * upv).astype(BF)
            hid[:, 0:256] = (hg * upv * s * (1.0 + gate * (1.0 - s))).astype(BF)
            hid[:, 256:512] = (hg * silu).astype(BF)

            def tile(n, _):
                cols = pl.ds(pl.multiple_of(n * WIDE, WIDE), WIDE)
                part[e, :, cols] = dot(hid[...], wgu[e, cols, :], TB).astype(BF)
                agu[e, cols, :] += dot(tok[e, :, cols], hid[...], TA)
                ad[e, :, cols] += dot(act[...], grad[e, :, cols], TA)
                return 0

            lax.fori_loop(0, 2048 // WIDE, tile, 0)
            return 0

        lax.fori_loop(0, 2, expert, 0)

        def sort_out(i, _):
            b, n = lax.div(i, 2), lax.rem(i, 2)
            rows = pl.ds(pl.multiple_of(b * MSG, MSG), MSG)
            lo = pl.ds(pl.multiple_of(n * WIDE, WIDE), WIDE)
            hi = pl.ds(pl.multiple_of(n * WIDE + 1024, WIDE), WIDE)
            v = jnp.concatenate([part[0, rows, lo], part[1, rows, lo], part[0, rows, hi], part[1, rows, hi]], axis=0)
            out[pl.ds(pl.multiple_of(h * HALF + b * BLK, BLK), BLK), lo] = dot(perm[...], v, AT).astype(BF)
            return 0

        lax.fori_loop(0, 8, sort_out, 0)

    def got_half(ref, h, sem):
        def one(k, _):
            got(ref, k, sem)
            return 0

        lax.fori_loop(4 * h, 4 * h + 4, one, 0)

    def give(k, _, buf=None, land=None, rsem=None, i=0, to=None):
        pltpu.make_async_remote_copy(block(buf, k), block(land, k), ret_s.at[i], rsem.at[k], device_id=to, device_id_type=MESH).start()
        return 0

    def give_down(h):
        lax.fori_loop(4 * h, 4 * h + 4, functools.partial(give, buf=p_below, land=ret_a, rsem=reta_r, i=0, to=down), 0)

    def give_up(h):
        lax.fori_loop(4 * h, 4 * h + 4, functools.partial(give, buf=p_above, land=ret_b, rsem=retb_r, i=1, to=up), 0)

    def settle(k, _):
        got(ret_a, k, reta_r)
        got(ret_b, k, retb_r)
        ca = pltpu.make_async_copy(block(ret_a, k), rstage.at[pl.ds(0, BLK)], st_s.at[0])
        cb = pltpu.make_async_copy(block(ret_b, k), rstage.at[pl.ds(BLK, BLK)], st_s.at[1])
        ca.start()
        cb.start()
        ca.wait()
        cb.wait()
        rows = pl.ds(pl.multiple_of(k * BLK, BLK), BLK)
        p_near[rows, :] = (p_near[rows, :].astype(F32) + rstage[0:BLK, :].astype(F32) + rstage[BLK : 2 * BLK, :].astype(F32)).astype(BF)
        send_block(k, p_near, back, back_s, back_r, k * BLK, -1, 1024)
        return 0

    def combine(k, _, buf=None, sem=None, m=None):
        got(buf, k, sem)
        cp = pltpu.make_async_copy(block(buf, k), rstage.at[pl.ds(0, BLK)], st_s.at[0])
        cp.start()
        want, q = rows_of(k)
        t0, t1 = m[0:1, :], m[1:2, :]
        lo = jnp.where(q < 24, jnp.where((want == t0) | (want == t1), 1.0, 0.0), 0.0).astype(BF)
        hi = jnp.where(q >= 24, jnp.where((want - 24.0 == t0) | (want - 24.0 == t1), 1.0, 0.0), 0.0).astype(BF)
        cp.wait()
        dacc[:, 0:1024] += dot(lo, rstage[0:BLK, :], TA)
        dacc[:, 1024:2048] += dot(hi, rstage[0:BLK, :], TA)
        return 0

    home = pltpu.make_async_remote_copy(dsend, dfar, dfar_s.at[0], dfar_r.at[0], device_id=over, device_id_type=MESH)
    mine = functools.partial(combine, buf=back, sem=back_r, m=meta)
    theirs = functools.partial(combine, buf=back_o, sem=backo_r, m=far_meta)

    def send_opp(k, _):
        send_block(k, p_opp, back_o, backo_s, backo_r, k * BLK, -1, 1024)
        return 0

    lax.fori_loop(0, 4, forward, 0)
    for cp in fars:
        cp.wait()
    dispatch(far, far_meta, msg_o, opp, opp_s, opp_r)
    compute(near, 0, p_near)
    lax.fori_loop(4, 8, forward, 0)
    compute(near, 1, p_near)

    got_half(below, 0, below_r)
    compute(below, 0, p_below)
    give_down(0)
    got_half(above, 0, above_r)
    compute(above, 0, p_above)
    give_up(0)

    got_half(opp, 0, opp_r)
    compute(opp, 0, p_opp)
    lax.fori_loop(0, 4, send_opp, 0)

    got_half(below, 1, below_r)
    compute(below, 1, p_below)
    give_down(1)
    got_half(above, 1, above_r)
    compute(above, 1, p_above)
    give_up(1)

    got_half(opp, 1, opp_r)
    compute(opp, 1, p_opp)
    lax.fori_loop(4, 8, send_opp, 0)

    outs = [
        pltpu.make_async_copy(agu.at[:, :, pl.ds(0, 256)], gg_out, out_s.at[0]),
        pltpu.make_async_copy(agu.at[:, :, pl.ds(256, 256)], gu_out, out_s.at[1]),
        pltpu.make_async_copy(ad, gd_out, out_s.at[2]),
    ]
    for cp in outs:
        cp.start()

    lax.fori_loop(0, 5, settle, 0)
    dacc[...] = jnp.zeros_like(dacc)
    lax.fori_loop(0, 8, theirs, 0)
    dsend[...] = dacc[...].astype(BF)
    home.start()
    dacc[...] = jnp.zeros_like(dacc)

    def both_ways(k, _):
        settle(k, 0)
        mine(2 * k - 10, 0)
        mine(2 * k - 9, 0)
        return 0

    lax.fori_loop(5, 7, both_ways, 0)
    settle(7, 0)
    lax.fori_loop(4, 8, mine, 0)
    home.wait()
    dout[...] = (dacc[...] + dfar[...].astype(F32)).astype(BF)
    last = pltpu.make_async_copy(dout, d_out, out_s.at[3])
    last.start()

    def sent(ref, rows, sem, i):
        pltpu.make_async_copy(ref.at[pl.ds(0, rows)], ref.at[pl.ds(0, rows)], sem.at[i]).wait()

    sent(near, 31 * MSG, near_s, 0)
    sent(opp, 31 * MSG, opp_s, 0)
    sent(near, ROWS, fwd_s, 0)
    sent(near, ROWS, fwd_s, 1)
    sent(ret_a, ROWS, ret_s, 0)
    sent(ret_b, ROWS, ret_s, 1)
    sent(back, 31 * MSG, back_s, 0)
    sent(back_o, 31 * MSG, backo_s, 0)
    for cp in outs:
        cp.wait()
    last.wait()


def body(tokens, out_grad, probs, ids, wg, wu, wd):
    meta = jnp.concatenate([ids.T.astype(F32), probs.T, jnp.zeros((4, 128), F32)], axis=0)
    hbm = pl.BlockSpec(memory_space=pltpu.HBM)
    vm = pl.BlockSpec(memory_space=pltpu.VMEM)
    sd = jax.ShapeDtypeStruct
    wide, slim = sd((ROWS, 2048), BF), sd((ROWS, 1024), BF)
    dma = pltpu.SemaphoreType.DMA
    outs = pl.pallas_call(
        kernel,
        name="expert_backward",
        out_shape=[
            sd((128, 2048), BF), sd((2, 2048, 256), F32), sd((2, 2048, 256), F32), sd((2, 256, 2048), F32),
            wide, wide, wide, wide, slim, slim, slim, slim,
        ],
        in_specs=[hbm, hbm, vm, hbm, hbm, hbm],
        out_specs=[hbm] * 12,
        scratch_shapes=[
            pltpu.VMEM((256, 2048), BF), pltpu.VMEM((256, 2048), BF), pltpu.VMEM((8, 128), F32), pltpu.VMEM((8, 128), F32),
            pltpu.VMEM((4 * BLK, 2048), BF), pltpu.VMEM((4 * BLK, 2048), BF), pltpu.VMEM((BLK, BLK), BF),
            pltpu.VMEM((HALF, 2048), BF), pltpu.VMEM((2, BLK, 2048), BF), pltpu.VMEM((2, BLK, 2048), BF),
            pltpu.VMEM((BLK, 256), BF), pltpu.VMEM((BLK, 512), BF), pltpu.VMEM((2, BLK, 2048), BF),
            pltpu.VMEM((ROWS, 1024), BF), pltpu.VMEM((ROWS, 1024), BF), pltpu.VMEM((ROWS, 1024), BF), pltpu.VMEM((ROWS, 1024), BF),
            pltpu.VMEM((2 * BLK, 1024), BF), pltpu.VMEM((128, 2048), F32), pltpu.VMEM((128, 2048), BF), pltpu.VMEM((128, 2048), BF),
            pltpu.VMEM((2, 2048, 512), BF), pltpu.VMEM((2, 256, 2048), BF),
            pltpu.VMEM((2, 2048, 512), F32), pltpu.VMEM((2, 256, 2048), F32), pltpu.VMEM((128, 2048), BF),
            dma((3,)), dma((3,)), dma((5,)), dma((1,)), dma((8,)), dma((1,)), dma((8,)), dma((2,)), dma((8,)), dma((8,)),
            dma((1,)), dma((2,)), dma((8,)), dma((8,)), dma((1,)), dma((8,)), dma((1,)), dma((8,)), dma((1,)), dma((1,)),
            dma((3,)), dma((4,)), dma((4,)),
        ],
        compiler_params=pltpu.CompilerParams(collective_id=0, has_side_effects=True, vmem_limit_bytes=62 * 2**20),
    )(tokens, out_grad, meta, wg, wu, wd)
    return tuple(outs[:4])


def solution(mesh):
    tok = P(("dp", "expert"), None)
    col, row = P("expert", None, "dp"), P("expert", "dp", None)
    return jax.shard_map(
        body, mesh=mesh, in_specs=(tok, tok, tok, tok, col, col, row), out_specs=(tok, col, col, row), check_vma=False
    )
```

```python
import functools

import jax
import jax.numpy as jnp
from jax import lax
from jax.experimental import pallas as pl
from jax.experimental.pallas import tpu as pltpu
from jax.sharding import PartitionSpec as P

MESH = pl.DeviceIdType.MESH
BF = jnp.bfloat16
F32 = jnp.float32
CAP = 12
MSG = 4 * CAP
BLK = 4 * MSG
HALF = 4 * BLK
ROWS = 8 * BLK
WIDE = 512
AT = ((1,), (0,))
TB = ((1,), (1,))
TA = ((0,), (0,))


def dot(a, b, dims):
    return lax.dot_general(a, b, (dims, ((), ())), preferred_element_type=F32)


def place():
    dp, ex = lax.axis_index("dp"), lax.axis_index("expert")
    return lax.rem(lax.div(ex, 2), 4), lax.rem(dp, 2) * 2 + lax.div(ex, 8), lax.div(dp, 2), lax.rem(ex, 2)


def device(x, y, z, c):
    return (z * 2 + lax.div(y, 2), lax.rem(y, 2) * 8 + x * 2 + c)


def kernel(
    tokens, out_grad, meta_in, wg_hbm, wu_hbm, wd_hbm,
    dout, agu, ad, near, above, below, opp, ret_a, ret_b, back, back_o,
    raw, raw_o, meta, meta_o, msg, perm, stage, tok, grad, act, hid, part, p_near, p_above, p_below, p_opp,
    rstage, dacc, dsend, dfar, wgu, wd,
    far_s, far_r, loc, ys, yr, yms, ymr, yos, yor, yoms, yomr, near_s, near_r, opp_s, opp_r, fwd_s, above_r, below_r, pa_s, ret_s, reta_r, retb_r,
    back_s, back_r, backo_s, backo_r, dfar_s, dfar_r, st_s, stage_s,
):
    x, y, z, c = place()
    up = device(x, y, lax.rem(z + 1, 4), c)
    down = device(x, y, lax.rem(z + 3, 4), c)
    over = device(x, y, lax.rem(z + 2, 4), c)

    def hop(j):
        return j + lax.div(j, 2) * (1 - 2 * lax.rem(j, 2))

    def peer(k, dx, sign):
        dy, dc = hop(lax.div(k, 2)), lax.rem(k, 2)
        return device(lax.rem(x + sign * dx + 4, 4), lax.rem(y + sign * dy + 4, 4), z, lax.rem(c + dc, 2))

    loads = [
        pltpu.make_async_copy(tokens, raw.at[0, pl.ds(0, 128)], loc.at[0]),
        pltpu.make_async_copy(out_grad, raw.at[0, pl.ds(128, 128)], loc.at[1]),
        pltpu.make_async_copy(wg_hbm, wgu.at[:, :, pl.ds(0, 256)], loc.at[2]),
        pltpu.make_async_copy(wu_hbm, wgu.at[:, :, pl.ds(256, 256)], loc.at[3]),
        pltpu.make_async_copy(wd_hbm, wd, loc.at[4]),
    ]
    for cp in loads:
        cp.start()

    barrier = pltpu.get_barrier_semaphore()
    for other in (up, down, over):
        pl.semaphore_signal(barrier, inc=1, device_id=other, device_id_type=MESH)

    def greet(s, _):
        pl.semaphore_signal(barrier, inc=1, device_id=peer(lax.div(s, 4), lax.rem(s, 4), 1), device_id_type=MESH)
        return 0

    lax.fori_loop(1, 32, greet, 0)

    e0, e1 = meta_in[0:1, :], meta_in[1:2, :]
    ei = lax.broadcasted_iota(jnp.int32, (32, 128), 0).astype(F32)
    h0, h1 = ei == e0, ei == e1
    before = (lax.broadcasted_iota(jnp.int32, (128, 128), 0) < lax.broadcasted_iota(jnp.int32, (128, 128), 1))
    counts = jnp.where(h0 | h1, 1.0, 0.0).astype(BF)
    earlier = dot(counts, jnp.where(before, 1.0, 0.0).astype(BF), AT)

    def row_of(hit, e):
        slot = jnp.sum(jnp.where(hit, earlier, 0.0), axis=0, keepdims=True)
        return 24.0 * e - 12.0 * (e - 2.0 * jnp.floor(e * 0.5)) + slot

    meta[0, 0:1, :] = row_of(h0, e0)
    meta[0, 1:2, :] = row_of(h1, e1)
    meta[0, 2:8, :] = meta_in[2:8, :]

    ri = lax.broadcasted_iota(jnp.int32, (BLK, BLK), 0)
    ci = lax.broadcasted_iota(jnp.int32, (BLK, BLK), 1)
    src = lax.div(lax.rem(ri, MSG), CAP) * MSG + lax.div(ri, MSG) * CAP + lax.rem(ri, CAP)
    perm[...] = jnp.where(ci == src, 1.0, 0.0).astype(BF)

    loads[0].wait()
    loads[1].wait()
    pl.semaphore_wait(barrier, 34)

    def remote(a, b, ss, rs, to):
        return pltpu.make_async_remote_copy(a, b, ss, rs, device_id=to, device_id_type=MESH)

    def along_y(rows, m, rs, rr, ms, mr):
        pairs = []
        for j, dy in ((1, 1), (2, 3), (3, 2)):
            to = device(x, lax.rem(y + dy, 4), z, c)
            pairs.append((remote(rows.at[0], rows.at[j], rs.at[j], rr.at[j], to), remote(m.at[0], m.at[j], ms.at[j], mr.at[j], to)))
        return pairs

    fars = [remote(meta.at[0], meta_o.at[0], far_s.at[1], far_r.at[1], over), remote(raw.at[0], raw_o.at[0], far_s.at[0], far_r.at[0], over)]
    sides = along_y(raw, meta, ys, yr, yms, ymr)
    sides_o = along_y(raw_o, meta_o, yos, yor, yoms, yomr)
    for a, b in sides:
        b.start()
        a.start()
    for cp in fars:
        cp.start()

    def rows_at(row, k):
        r = lax.broadcasted_iota(jnp.int32, (BLK, 1), 0)
        q, dx = lax.rem(r, MSG), lax.div(r, MSG)
        column = lax.rem(row, 2) * 8 + lax.rem(x + dx, 4) * 2 + lax.rem(c + lax.rem(k, 2), 2)
        return (column * MSG + q).astype(F32), q

    def build(rows, m, j, g):
        want, q = rows_at(y, g)
        t0, t1, p0, p1 = m[j, 0:1, :], m[j, 1:2, :], m[j, 2:3, :], m[j, 3:4, :]
        hit_t = (want == t0) | (want == t1)
        hit0, hit1 = want - 24.0 == t0, want - 24.0 == t1
        hit_t = jnp.where(q < 24, jnp.where(hit_t, 1.0, 0.0), 0.0)
        hit0 = jnp.where(q >= 24, jnp.where(hit0, 1.0, 0.0), 0.0)
        hit1 = jnp.where(q >= 24, jnp.where(hit1, 1.0, 0.0), 0.0)
        pick = jnp.concatenate([hit_t, hit0 + hit1], axis=1).astype(BF)
        scale = jnp.sum(hit0 * p0 + hit1 * p1, axis=1, keepdims=True) + jnp.where(q < 24, 1.0, 0.0)
        base = pl.multiple_of(g * BLK, BLK)

        def part_of(n, _):
            cols = pl.ds(pl.multiple_of(n * WIDE, WIDE), WIDE)
            msg[pl.ds(base, BLK), cols] = (dot(pick, rows[j, :, cols], AT) * scale).astype(BF)
            return 0

        lax.fori_loop(0, 2048 // WIDE, part_of, 0)

    def send_block(k, src_buf, dst_buf, ssem, rsem, base, sign, width):
        for dx in range(4):
            frm = src_buf.at[pl.ds(pl.multiple_of(base + dx * MSG, MSG), MSG), pl.ds(0, width)]
            to = dst_buf.at[pl.ds(pl.multiple_of(k * BLK + dx * MSG, MSG), MSG), pl.ds(0, width)]
            if dx == 0:
                @pl.when(k == 0)
                def _():
                    pltpu.make_async_copy(frm, to, rsem.at[k]).start()

                @pl.when(k > 0)
                def _():
                    pltpu.make_async_remote_copy(frm, to, ssem.at[0], rsem.at[k], device_id=peer(k, dx, sign), device_id_type=MESH).start()
            else:
                pltpu.make_async_remote_copy(frm, to, ssem.at[0], rsem.at[k], device_id=peer(k, dx, sign), device_id_type=MESH).start()

    def block(ref, k):
        return ref.at[pl.ds(pl.multiple_of(k * BLK, BLK), BLK)]

    def got(ref, k, sem):
        pltpu.make_async_copy(block(ref, k), block(ref, k), sem.at[k]).wait()

    def leave(k, dst, ssem, rsem):
        own = lax.rem(k, 2)
        for dx in range(4):
            at = pl.ds(pl.multiple_of(k * BLK + dx * MSG, MSG), MSG)
            to = device(lax.rem(x + dx, 4), y, z, lax.rem(c + own, 2))
            if dx == 0:
                @pl.when(own == 0)
                def _():
                    pltpu.make_async_copy(msg.at[at], dst.at[at], rsem.at[k]).start()

                @pl.when(own == 1)
                def _():
                    remote(msg.at[at], dst.at[at], ssem.at[k], rsem.at[k], to).start()
            else:
                remote(msg.at[at], dst.at[at], ssem.at[k], rsem.at[k], to).start()

    def left(k, ssem):
        three, one = near.at[pl.ds(0, 3 * MSG)], near.at[pl.ds(0, MSG)]
        pltpu.make_async_copy(three, three, ssem.at[k]).wait()

        @pl.when(lax.rem(k, 2) == 1)
        def _():
            pltpu.make_async_copy(one, one, ssem.at[k]).wait()

    def dispatch(j):
        if j:
            sides[j - 1][0].wait_recv()
            sides[j - 1][1].wait_recv()

        def one(k, _):
            build(raw, meta, j, k)
            leave(k, near, near_s, near_r)
            return 0

        lax.fori_loop(2 * j, 2 * j + 2, one, 0)

    def dispatch_o(j):
        if j:
            sides_o[j - 1][0].wait_recv()
            sides_o[j - 1][1].wait_recv()

        def one(k, _):
            left(k, near_s)
            build(raw_o, meta_o, j, k)
            leave(k, opp, opp_s, opp_r)
            return 0

        lax.fori_loop(2 * j, 2 * j + 2, one, 0)

    dispatch(0)

    def clear(n, _):
        rows = pl.ds(pl.multiple_of(n * 256, 256), 256)
        for e in range(2):
            agu[e, rows, :] = jnp.zeros((256, 512), F32)
        return 0

    lax.fori_loop(0, 8, clear, 0)

    def clear_d(n, _):
        cols = pl.ds(pl.multiple_of(n * 256, 256), 256)
        for e in range(2):
            ad[e, :, cols] = jnp.zeros((256, 256), F32)
        return 0

    lax.fori_loop(0, 8, clear_d, 0)
    for cp in loads[2:]:
        cp.wait()

    def forward(k, _):
        got(near, k, near_r)
        pltpu.make_async_remote_copy(block(near, k), block(below, k), fwd_s.at[0], below_r.at[k], device_id=up, device_id_type=MESH).start()
        pltpu.make_async_remote_copy(block(near, k), block(above, k), fwd_s.at[1], above_r.at[k], device_id=down, device_id_type=MESH).start()
        return 0

    def load(buf, h, b):
        return pltpu.make_async_copy(
            buf.at[pl.ds(pl.multiple_of(h * HALF + b * BLK, BLK), BLK)], stage.at[pl.ds(pl.multiple_of(b * BLK, BLK), BLK)], stage_s.at[b]
        )

    def compute(buf, h, out):
        for b in range(4):
            load(buf, h, b).start()

        def sort_in(i, _):
            b, n = lax.div(i, 4), lax.rem(i, 4)

            @pl.when(n == 0)
            def _():
                load(buf, h, b).wait()

            cols = pl.ds(pl.multiple_of(n * WIDE, WIDE), WIDE)
            v = dot(perm[...], stage[pl.ds(pl.multiple_of(b * BLK, BLK), BLK), cols], AT).astype(BF)
            rows = pl.ds(pl.multiple_of(b * MSG, MSG), MSG)
            tok[0, rows, cols] = v[0:48]
            tok[1, rows, cols] = v[48:96]
            grad[0, rows, cols] = v[96:144]
            grad[1, rows, cols] = v[144:192]
            return 0

        lax.fori_loop(0, 16, sort_in, 0)

        def expert(e, _):
            gate = dot(tok[e], wgu[e, :, 0:256], AT)
            upv = dot(tok[e], wgu[e, :, 256:512], AT)
            hg = dot(grad[e], wd[e], TB)
            s = jax.nn.sigmoid(gate)
            silu = gate * s
            act[...] = (silu * upv).astype(BF)
            hid[:, 0:256] = (hg * upv * s * (1.0 + gate * (1.0 - s))).astype(BF)
            hid[:, 256:512] = (hg * silu).astype(BF)

            def tile(n, _):
                cols = pl.ds(pl.multiple_of(n * WIDE, WIDE), WIDE)
                part[e, :, cols] = dot(hid[...], wgu[e, cols, :], TB).astype(BF)
                agu[e, cols, :] += dot(tok[e, :, cols], hid[...], TA)
                ad[e, :, cols] += dot(act[...], grad[e, :, cols], TA)
                return 0

            lax.fori_loop(0, 2048 // WIDE, tile, 0)
            return 0

        lax.fori_loop(0, 2, expert, 0)

        def sort_out(i, _):
            b, n = lax.div(i, 2), lax.rem(i, 2)
            rows = pl.ds(pl.multiple_of(b * MSG, MSG), MSG)
            lo = pl.ds(pl.multiple_of(n * WIDE, WIDE), WIDE)
            hi = pl.ds(pl.multiple_of(n * WIDE + 1024, WIDE), WIDE)
            v = jnp.concatenate([part[0, rows, lo], part[1, rows, lo], part[0, rows, hi], part[1, rows, hi]], axis=0)
            out[pl.ds(pl.multiple_of(h * HALF + b * BLK, BLK), BLK), lo] = dot(perm[...], v, AT).astype(BF)
            return 0

        lax.fori_loop(0, 8, sort_out, 0)

    def got_half(ref, h, sem):
        def one(k, _):
            got(ref, k, sem)
            return 0

        lax.fori_loop(4 * h, 4 * h + 4, one, 0)

    def give(k, _, buf=None, land=None, rsem=None, i=0, to=None):
        pltpu.make_async_remote_copy(block(buf, k), block(land, k), ret_s.at[i], rsem.at[k], device_id=to, device_id_type=MESH).start()
        return 0

    def give_down(h):
        lax.fori_loop(4 * h, 4 * h + 4, functools.partial(give, buf=p_below, land=ret_a, rsem=reta_r, i=0, to=down), 0)

    def give_up(h):
        lax.fori_loop(4 * h, 4 * h + 4, functools.partial(give, buf=p_above, land=ret_b, rsem=retb_r, i=1, to=up), 0)

    def settle(k, _):
        got(ret_a, k, reta_r)
        got(ret_b, k, retb_r)
        ca = pltpu.make_async_copy(block(ret_a, k), rstage.at[pl.ds(0, BLK)], st_s.at[0])
        cb = pltpu.make_async_copy(block(ret_b, k), rstage.at[pl.ds(BLK, BLK)], st_s.at[1])
        ca.start()
        cb.start()
        ca.wait()
        cb.wait()
        rows = pl.ds(pl.multiple_of(k * BLK, BLK), BLK)
        p_near[rows, :] = (p_near[rows, :].astype(F32) + rstage[0:BLK, :].astype(F32) + rstage[BLK : 2 * BLK, :].astype(F32)).astype(BF)
        send_block(k, p_near, back, back_s, back_r, k * BLK, -1, 1024)
        return 0

    def combine(k, _, buf=None, sem=None, m=None):
        got(buf, k, sem)
        cp = pltpu.make_async_copy(block(buf, k), rstage.at[pl.ds(0, BLK)], st_s.at[0])
        cp.start()
        want, q = rows_at(y + hop(lax.div(k, 2)), k)
        t0, t1 = m[0, 0:1, :], m[0, 1:2, :]
        lo = jnp.where(q < 24, jnp.where((want == t0) | (want == t1), 1.0, 0.0), 0.0).astype(BF)
        hi = jnp.where(q >= 24, jnp.where((want - 24.0 == t0) | (want - 24.0 == t1), 1.0, 0.0), 0.0).astype(BF)
        cp.wait()
        dacc[:, 0:1024] += dot(lo, rstage[0:BLK, :], TA)
        dacc[:, 1024:2048] += dot(hi, rstage[0:BLK, :], TA)
        return 0

    home = pltpu.make_async_remote_copy(dsend, dfar, dfar_s.at[0], dfar_r.at[0], device_id=over, device_id_type=MESH)
    mine = functools.partial(combine, buf=back, sem=back_r, m=meta)
    theirs = functools.partial(combine, buf=back_o, sem=backo_r, m=meta_o)

    def send_opp(k, _):
        send_block(k, p_opp, back_o, backo_s, backo_r, k * BLK, -1, 1024)
        return 0

    lax.fori_loop(0, 2, forward, 0)
    dispatch(1)
    dispatch(2)
    for cp in fars:
        cp.wait_recv()
    for a, b in sides_o:
        b.start()
        a.start()
    dispatch(3)
    lax.fori_loop(2, 4, forward, 0)
    compute(near, 0, p_near)
    lax.fori_loop(4, 6, forward, 0)
    dispatch_o(0)
    lax.fori_loop(6, 8, forward, 0)
    dispatch_o(1)
    dispatch_o(2)
    dispatch_o(3)
    compute(near, 1, p_near)

    got_half(below, 0, below_r)
    compute(below, 0, p_below)
    give_down(0)
    got_half(above, 0, above_r)
    compute(above, 0, p_above)
    give_up(0)

    got_half(opp, 0, opp_r)
    compute(opp, 0, p_opp)
    lax.fori_loop(0, 4, send_opp, 0)

    got_half(opp, 1, opp_r)
    compute(opp, 1, p_opp)
    lax.fori_loop(4, 8, send_opp, 0)

    got_half(below, 1, below_r)
    compute(below, 1, p_below)
    give_down(1)
    got_half(above, 1, above_r)
    compute(above, 1, p_above)
    give_up(1)

    lax.fori_loop(0, 4, settle, 0)
    dacc[...] = jnp.zeros_like(dacc)
    lax.fori_loop(0, 8, theirs, 0)
    dsend[...] = dacc[...].astype(BF)
    home.start()
    dacc[...] = jnp.zeros_like(dacc)

    def both_ways(k, _):
        settle(k, 0)
        mine(2 * k - 8, 0)
        mine(2 * k - 7, 0)
        return 0

    lax.fori_loop(4, 6, both_ways, 0)
    lax.fori_loop(6, 8, settle, 0)
    lax.fori_loop(4, 8, mine, 0)
    home.wait()
    dout[...] = (dacc[...] + dfar[...].astype(F32)).astype(BF)

    def sent(ref, rows, sem, i):
        pltpu.make_async_copy(ref.at[pl.ds(0, rows)], ref.at[pl.ds(0, rows)], sem.at[i]).wait()

    def last_left(k, _):
        left(k, opp_s)
        return 0

    lax.fori_loop(0, 8, last_left, 0)
    for cp in fars:
        cp.wait_send()
    for a, b in sides + sides_o:
        a.wait_send()
        b.wait_send()
    sent(near, ROWS, fwd_s, 0)
    sent(near, ROWS, fwd_s, 1)
    sent(ret_a, ROWS, ret_s, 0)
    sent(ret_b, ROWS, ret_s, 1)
    sent(back, 31 * MSG, back_s, 0)
    sent(back_o, 31 * MSG, backo_s, 0)


def body(tokens, out_grad, probs, ids, wg, wu, wd):
    meta = jnp.concatenate([ids.T.astype(F32), probs.T, jnp.zeros((4, 128), F32)], axis=0)
    hbm = pl.BlockSpec(memory_space=pltpu.HBM)
    vm = pl.BlockSpec(memory_space=pltpu.VMEM)
    sd = jax.ShapeDtypeStruct
    wide, slim = sd((ROWS, 2048), BF), sd((ROWS, 1024), BF)
    dma = pltpu.SemaphoreType.DMA
    outs = pl.pallas_call(
        kernel,
        name="expert_backward",
        out_shape=[
            pltpu.VMEM((128, 2048), BF), pltpu.VMEM((2, 2048, 512), F32), pltpu.VMEM((2, 256, 2048), F32),
            wide, wide, wide, wide, slim, slim, slim, slim,
        ],
        in_specs=[hbm, hbm, vm, hbm, hbm, hbm],
        out_specs=[vm] * 3 + [hbm] * 8,
        scratch_shapes=[
            pltpu.VMEM((4, 256, 2048), BF), pltpu.VMEM((4, 256, 2048), BF), pltpu.VMEM((4, 8, 128), F32), pltpu.VMEM((4, 8, 128), F32),
            pltpu.VMEM((ROWS, 2048), BF), pltpu.VMEM((BLK, BLK), BF),
            pltpu.VMEM((HALF, 2048), BF), pltpu.VMEM((2, BLK, 2048), BF), pltpu.VMEM((2, BLK, 2048), BF),
            pltpu.VMEM((BLK, 256), BF), pltpu.VMEM((BLK, 512), BF), pltpu.VMEM((2, BLK, 2048), BF),
            pltpu.VMEM((ROWS, 1024), BF), pltpu.VMEM((ROWS, 1024), BF), pltpu.VMEM((ROWS, 1024), BF), pltpu.VMEM((ROWS, 1024), BF),
            pltpu.VMEM((2 * BLK, 1024), BF), pltpu.VMEM((128, 2048), F32), pltpu.VMEM((128, 2048), BF), pltpu.VMEM((128, 2048), BF),
            pltpu.VMEM((2, 2048, 512), BF), pltpu.VMEM((2, 256, 2048), BF),
            dma((2,)), dma((2,)), dma((5,)), *[dma((4,))] * 8, dma((8,)), dma((8,)), dma((8,)), dma((8,)), dma((2,)), dma((8,)), dma((8,)),
            dma((1,)), dma((2,)), dma((8,)), dma((8,)), dma((1,)), dma((8,)), dma((1,)), dma((8,)), dma((1,)), dma((1,)),
            dma((3,)), dma((4,)),
        ],
        compiler_params=pltpu.CompilerParams(collective_id=0, has_side_effects=True, vmem_limit_bytes=46 * 2**20),
    )(tokens, out_grad, meta, wg, wu, wd)
    d, gu, gd = outs[:3]
    return d, gu[:, :, :256], gu[:, :, 256:], gd


def solution(mesh):
    tok = P(("dp", "expert"), None)
    col, row = P("expert", None, "dp"), P("expert", "dp", None)
    return jax.shard_map(
        body, mesh=mesh, in_specs=(tok, tok, tok, tok, col, col, row), out_specs=(tok, col, col, row), check_vma=False
    )
```

```python
import functools

import jax
import jax.numpy as jnp
from jax import lax
from jax.experimental import pallas as pl
from jax.experimental.pallas import tpu as pltpu
from jax.sharding import PartitionSpec as P

MESH = pl.DeviceIdType.MESH
BF = jnp.bfloat16
F32 = jnp.float32
CAP = 12
MSG = 4 * CAP
BLK = 4 * MSG
HALF = 4 * BLK
ROWS = 8 * BLK
WIDE = 512
AT = ((1,), (0,))
TB = ((1,), (1,))
TA = ((0,), (0,))


def dot(a, b, dims):
    return lax.dot_general(a, b, (dims, ((), ())), preferred_element_type=F32)


def place():
    dp, ex = lax.axis_index("dp"), lax.axis_index("expert")
    return lax.rem(lax.div(ex, 2), 4), lax.rem(dp, 2) * 2 + lax.div(ex, 8), lax.div(dp, 2), lax.rem(ex, 2)


def device(x, y, z, c):
    return (z * 2 + lax.div(y, 2), lax.rem(y, 2) * 8 + x * 2 + c)


def kernel(
    tokens, out_grad, ids, probs, wg_hbm, wu_hbm, wd_hbm,
    dout, agu, ad, near, above, below, opp, ret_a, ret_b, back, back_o,
    raw, raw_o, meta, meta_o, msg, perm, stage, tok, grad, act, hid, part, p_near, p_above, p_below, p_opp,
    rstage, dacc, dsend, dfar, wgu, wd,
    far_s, far_r, loc, ys, yr, yms, ymr, yos, yor, yoms, yomr, near_s, near_r, opp_s, opp_r, fwd_s, above_r, below_r, pa_s, ret_s, reta_r, retb_r,
    back_s, back_r, backo_s, backo_r, dfar_s, dfar_r, st_s, stage_s, side_s,
):
    x, y, z, c = place()
    up = device(x, y, lax.rem(z + 1, 4), c)
    down = device(x, y, lax.rem(z + 3, 4), c)
    over = device(x, y, lax.rem(z + 2, 4), c)

    def hop(j):
        return j + lax.div(j, 2) * (1 - 2 * lax.rem(j, 2))

    def peer(k, dx, sign):
        dy, dc = hop(lax.div(k, 2)), lax.rem(k, 2)
        return device(lax.rem(x + sign * dx + 4, 4), lax.rem(y + sign * dy + 4, 4), z, lax.rem(c + dc, 2))

    loads = [
        pltpu.make_async_copy(tokens, raw.at[0, pl.ds(0, 128)], loc.at[0]),
        pltpu.make_async_copy(out_grad, raw.at[0, pl.ds(128, 128)], loc.at[1]),
        pltpu.make_async_copy(wg_hbm, wgu.at[:, :, pl.ds(0, 256)], loc.at[2]),
        pltpu.make_async_copy(wu_hbm, wgu.at[:, :, pl.ds(256, 256)], loc.at[3]),
        pltpu.make_async_copy(wd_hbm, wd, loc.at[4]),
    ]
    for cp in loads:
        cp.start()

    barrier = pltpu.get_barrier_semaphore()
    for other in (up, down, over):
        pl.semaphore_signal(barrier, inc=1, device_id=other, device_id_type=MESH)

    def greet(s, _):
        pl.semaphore_signal(barrier, inc=1, device_id=peer(lax.div(s, 4), lax.rem(s, 4), 1), device_id_type=MESH)
        return 0

    lax.fori_loop(1, 32, greet, 0)

    e0, e1 = ids[0:1, :].astype(F32), ids[1:2, :].astype(F32)
    ei = lax.broadcasted_iota(jnp.int32, (32, 128), 0).astype(F32)
    h0, h1 = ei == e0, ei == e1
    before = (lax.broadcasted_iota(jnp.int32, (128, 128), 0) < lax.broadcasted_iota(jnp.int32, (128, 128), 1))
    counts = jnp.where(h0 | h1, 1.0, 0.0).astype(BF)
    earlier = dot(counts, jnp.where(before, 1.0, 0.0).astype(BF), AT)

    def row_of(hit, e):
        slot = jnp.sum(jnp.where(hit, earlier, 0.0), axis=0, keepdims=True)
        return 24.0 * e - 12.0 * (e - 2.0 * jnp.floor(e * 0.5)) + slot

    meta[0, 0:1, :] = row_of(h0, e0)
    meta[0, 1:2, :] = row_of(h1, e1)
    meta[0, 2:4, :] = probs[...]
    meta[0, 4:8, :] = jnp.zeros((4, 128), F32)

    ri = lax.broadcasted_iota(jnp.int32, (BLK, BLK), 0)
    ci = lax.broadcasted_iota(jnp.int32, (BLK, BLK), 1)
    src = lax.div(lax.rem(ri, MSG), CAP) * MSG + lax.div(ri, MSG) * CAP + lax.rem(ri, CAP)
    perm[...] = jnp.where(ci == src, 1.0, 0.0).astype(BF)

    loads[0].wait()
    loads[1].wait()
    pl.semaphore_wait(barrier, 34)

    def remote(a, b, ss, rs, to):
        return pltpu.make_async_remote_copy(a, b, ss, rs, device_id=to, device_id_type=MESH)

    def along_y(rows, m, rs, rr, ms, mr):
        pairs = []
        for j, dy in ((1, 1), (2, 3), (3, 2)):
            to = device(x, lax.rem(y + dy, 4), z, c)
            pairs.append((remote(rows.at[0], rows.at[j], rs.at[j], rr.at[j], to), remote(m.at[0], m.at[j], ms.at[j], mr.at[j], to)))
        return pairs

    fars = [remote(meta.at[0], meta_o.at[0], far_s.at[1], far_r.at[1], over), remote(raw.at[0], raw_o.at[0], far_s.at[0], far_r.at[0], over)]
    sides = along_y(raw, meta, ys, yr, yms, ymr)
    sides_o = along_y(raw_o, meta_o, yos, yor, yoms, yomr)
    for a, b in sides:
        b.start()
        a.start()
    for cp in fars:
        cp.start()

    def rows_at(row, k):
        r = lax.broadcasted_iota(jnp.int32, (BLK, 1), 0)
        q, dx = lax.rem(r, MSG), lax.div(r, MSG)
        column = lax.rem(row, 2) * 8 + lax.rem(x + dx, 4) * 2 + lax.rem(c + lax.rem(k, 2), 2)
        return (column * MSG + q).astype(F32), q

    def build(rows, m, j, g):
        want, q = rows_at(y, g)
        t0, t1, p0, p1 = m[j, 0:1, :], m[j, 1:2, :], m[j, 2:3, :], m[j, 3:4, :]
        hit_t = (want == t0) | (want == t1)
        hit0, hit1 = want - 24.0 == t0, want - 24.0 == t1
        hit_t = jnp.where(q < 24, jnp.where(hit_t, 1.0, 0.0), 0.0)
        hit0 = jnp.where(q >= 24, jnp.where(hit0, 1.0, 0.0), 0.0)
        hit1 = jnp.where(q >= 24, jnp.where(hit1, 1.0, 0.0), 0.0)
        pick = jnp.concatenate([hit_t, hit0 + hit1], axis=1).astype(BF)
        scale = jnp.sum(hit0 * p0 + hit1 * p1, axis=1, keepdims=True) + jnp.where(q < 24, 1.0, 0.0)
        base = pl.multiple_of(g * BLK, BLK)

        def part_of(n, _):
            cols = pl.ds(pl.multiple_of(n * WIDE, WIDE), WIDE)
            msg[pl.ds(base, BLK), cols] = (dot(pick, rows[j, :, cols], AT) * scale).astype(BF)
            return 0

        lax.fori_loop(0, 2048 // WIDE, part_of, 0)

    def send_block(k, src_buf, dst_buf, ssem, rsem, base, sign, width):
        for dx in range(4):
            frm = src_buf.at[pl.ds(pl.multiple_of(base + dx * MSG, MSG), MSG), pl.ds(0, width)]
            to = dst_buf.at[pl.ds(pl.multiple_of(k * BLK + dx * MSG, MSG), MSG), pl.ds(0, width)]
            if dx == 0:
                @pl.when(k == 0)
                def _():
                    pltpu.make_async_copy(frm, to, rsem.at[k]).start()

                @pl.when(k > 0)
                def _():
                    pltpu.make_async_remote_copy(frm, to, ssem.at[0], rsem.at[k], device_id=peer(k, dx, sign), device_id_type=MESH).start()
            else:
                pltpu.make_async_remote_copy(frm, to, ssem.at[0], rsem.at[k], device_id=peer(k, dx, sign), device_id_type=MESH).start()

    def block(ref, k):
        return ref.at[pl.ds(pl.multiple_of(k * BLK, BLK), BLK)]

    def got(ref, k, sem):
        pltpu.make_async_copy(block(ref, k), block(ref, k), sem.at[k]).wait()

    def leave(k, dst, ssem, rsem):
        own = lax.rem(k, 2)
        for dx in range(4):
            at = pl.ds(pl.multiple_of(k * BLK + dx * MSG, MSG), MSG)
            to = device(lax.rem(x + dx, 4), y, z, lax.rem(c + own, 2))
            if dx == 0:
                @pl.when(own == 0)
                def _():
                    pltpu.make_async_copy(msg.at[at], dst.at[at], rsem.at[k]).start()

                @pl.when(own == 1)
                def _():
                    remote(msg.at[at], dst.at[at], ssem.at[k], rsem.at[k], to).start()
            else:
                remote(msg.at[at], dst.at[at], ssem.at[k], rsem.at[k], to).start()

    def left(k, ssem):
        three, one = near.at[pl.ds(0, 3 * MSG)], near.at[pl.ds(0, MSG)]
        pltpu.make_async_copy(three, three, ssem.at[k]).wait()

        @pl.when(lax.rem(k, 2) == 1)
        def _():
            pltpu.make_async_copy(one, one, ssem.at[k]).wait()

    def dispatch(j):
        if j:
            sides[j - 1][0].wait_recv()
            sides[j - 1][1].wait_recv()

        def one(k, _):
            build(raw, meta, j, k)
            leave(k, near, near_s, near_r)
            return 0

        lax.fori_loop(2 * j, 2 * j + 2, one, 0)

    def dispatch_o(j):
        if j:
            sides_o[j - 1][0].wait_recv()
            sides_o[j - 1][1].wait_recv()

        def one(k, _):
            left(k, near_s)
            build(raw_o, meta_o, j, k)
            leave(k, opp, opp_s, opp_r)
            return 0

        lax.fori_loop(2 * j, 2 * j + 2, one, 0)

    dispatch(0)

    def clear(n, _):
        rows = pl.ds(pl.multiple_of(n * 256, 256), 256)
        for e in range(2):
            agu[e, rows, :] = jnp.zeros((256, 512), F32)
        return 0

    lax.fori_loop(0, 8, clear, 0)

    def clear_d(n, _):
        cols = pl.ds(pl.multiple_of(n * 256, 256), 256)
        for e in range(2):
            ad[e, :, cols] = jnp.zeros((256, 256), F32)
        return 0

    lax.fori_loop(0, 8, clear_d, 0)
    for cp in loads[2:]:
        cp.wait()

    def forward(k, _):
        got(near, k, near_r)
        pltpu.make_async_remote_copy(block(near, k), block(below, k), fwd_s.at[0], below_r.at[k], device_id=up, device_id_type=MESH).start()
        pltpu.make_async_remote_copy(block(near, k), block(above, k), fwd_s.at[1], above_r.at[k], device_id=down, device_id_type=MESH).start()
        return 0

    across = device(x, lax.rem(y + 2, 4), z, c)

    def relay(k):
        got(below, k, below_r)
        got(above, k, above_r)
        remote(block(below, k), block(below, k + 6), side_s.at[0], below_r.at[k + 6], across).start()
        remote(block(above, k), block(above, k + 6), side_s.at[1], above_r.at[k + 6], across).start()

    def arrived(k, _):
        got(near, k, near_r)
        return 0

    def load(buf, h, b):
        return pltpu.make_async_copy(
            buf.at[pl.ds(pl.multiple_of(h * HALF + b * BLK, BLK), BLK)], stage.at[pl.ds(pl.multiple_of(b * BLK, BLK), BLK)], stage_s.at[b]
        )

    def compute(buf, h, out):
        for b in range(4):
            load(buf, h, b).start()

        def sort_in(i, _):
            b, n = lax.div(i, 4), lax.rem(i, 4)

            @pl.when(n == 0)
            def _():
                load(buf, h, b).wait()

            cols = pl.ds(pl.multiple_of(n * WIDE, WIDE), WIDE)
            v = dot(perm[...], stage[pl.ds(pl.multiple_of(b * BLK, BLK), BLK), cols], AT).astype(BF)
            rows = pl.ds(pl.multiple_of(b * MSG, MSG), MSG)
            tok[0, rows, cols] = v[0:48]
            tok[1, rows, cols] = v[48:96]
            grad[0, rows, cols] = v[96:144]
            grad[1, rows, cols] = v[144:192]
            return 0

        lax.fori_loop(0, 16, sort_in, 0)

        def expert(e, _):
            gate = dot(tok[e], wgu[e, :, 0:256], AT)
            upv = dot(tok[e], wgu[e, :, 256:512], AT)
            hg = dot(grad[e], wd[e], TB)
            s = jax.nn.sigmoid(gate)
            silu = gate * s
            act[...] = (silu * upv).astype(BF)
            hid[:, 0:256] = (hg * upv * s * (1.0 + gate * (1.0 - s))).astype(BF)
            hid[:, 256:512] = (hg * silu).astype(BF)

            def tile(n, _):
                cols = pl.ds(pl.multiple_of(n * WIDE, WIDE), WIDE)
                part[e, :, cols] = dot(hid[...], wgu[e, cols, :], TB).astype(BF)
                agu[e, cols, :] += dot(tok[e, :, cols], hid[...], TA)
                ad[e, :, cols] += dot(act[...], grad[e, :, cols], TA)
                return 0

            lax.fori_loop(0, 2048 // WIDE, tile, 0)
            return 0

        lax.fori_loop(0, 2, expert, 0)

        def sort_out(i, _):
            b, n = lax.div(i, 2), lax.rem(i, 2)
            rows = pl.ds(pl.multiple_of(b * MSG, MSG), MSG)
            lo = pl.ds(pl.multiple_of(n * WIDE, WIDE), WIDE)
            hi = pl.ds(pl.multiple_of(n * WIDE + 1024, WIDE), WIDE)
            v = jnp.concatenate([part[0, rows, lo], part[1, rows, lo], part[0, rows, hi], part[1, rows, hi]], axis=0)
            out[pl.ds(pl.multiple_of(h * HALF + b * BLK, BLK), BLK), lo] = dot(perm[...], v, AT).astype(BF)
            return 0

        lax.fori_loop(0, 8, sort_out, 0)

    def got_half(ref, h, sem, first=0):
        def one(k, _):
            got(ref, k, sem)
            return 0

        lax.fori_loop(4 * h + first, 4 * h + 4, one, 0)

    def give(k, _, buf=None, land=None, rsem=None, i=0, to=None):
        pltpu.make_async_remote_copy(block(buf, k), block(land, k), ret_s.at[i], rsem.at[k], device_id=to, device_id_type=MESH).start()
        return 0

    def give_down(h):
        lax.fori_loop(4 * h, 4 * h + 4, functools.partial(give, buf=p_below, land=ret_a, rsem=reta_r, i=0, to=down), 0)

    def give_up(h):
        lax.fori_loop(4 * h, 4 * h + 4, functools.partial(give, buf=p_above, land=ret_b, rsem=retb_r, i=1, to=up), 0)

    def settle(k, _):
        got(ret_a, k, reta_r)
        got(ret_b, k, retb_r)
        ca = pltpu.make_async_copy(block(ret_a, k), rstage.at[pl.ds(0, BLK)], st_s.at[0])
        cb = pltpu.make_async_copy(block(ret_b, k), rstage.at[pl.ds(BLK, BLK)], st_s.at[1])
        ca.start()
        cb.start()
        ca.wait()
        cb.wait()
        rows = pl.ds(pl.multiple_of(k * BLK, BLK), BLK)
        p_near[rows, :] = (p_near[rows, :].astype(F32) + rstage[0:BLK, :].astype(F32) + rstage[BLK : 2 * BLK, :].astype(F32)).astype(BF)
        send_block(k, p_near, back, back_s, back_r, k * BLK, -1, 1024)
        return 0

    def combine(k, _, buf=None, sem=None, m=None):
        got(buf, k, sem)
        cp = pltpu.make_async_copy(block(buf, k), rstage.at[pl.ds(0, BLK)], st_s.at[0])
        cp.start()
        want, q = rows_at(y + hop(lax.div(k, 2)), k)
        t0, t1 = m[0, 0:1, :], m[0, 1:2, :]
        lo = jnp.where(q < 24, jnp.where((want == t0) | (want == t1), 1.0, 0.0), 0.0).astype(BF)
        hi = jnp.where(q >= 24, jnp.where((want - 24.0 == t0) | (want - 24.0 == t1), 1.0, 0.0), 0.0).astype(BF)
        cp.wait()
        dacc[:, 0:1024] += dot(lo, rstage[0:BLK, :], TA)
        dacc[:, 1024:2048] += dot(hi, rstage[0:BLK, :], TA)
        return 0

    home = pltpu.make_async_remote_copy(dsend, dfar, dfar_s.at[0], dfar_r.at[0], device_id=over, device_id_type=MESH)
    mine = functools.partial(combine, buf=back, sem=back_r, m=meta)
    theirs = functools.partial(combine, buf=back_o, sem=backo_r, m=meta_o)

    def send_opp(k, _):
        send_block(k, p_opp, back_o, backo_s, backo_r, k * BLK, -1, 1024)
        return 0

    lax.fori_loop(0, 2, forward, 0)
    dispatch(1)
    dispatch(2)
    for cp in fars:
        cp.wait_recv()
    for a, b in sides_o:
        b.start()
        a.start()
    dispatch(3)
    lax.fori_loop(2, 4, forward, 0)
    compute(near, 0, p_near)
    relay(0)
    lax.fori_loop(4, 6, forward, 0)
    dispatch_o(0)
    relay(1)
    lax.fori_loop(6, 8, arrived, 0)
    dispatch_o(1)
    dispatch_o(2)
    dispatch_o(3)
    compute(near, 1, p_near)

    got_half(below, 0, below_r, 2)
    compute(below, 0, p_below)
    got_half(above, 0, above_r, 2)
    compute(above, 0, p_above)

    got_half(opp, 0, opp_r)
    compute(opp, 0, p_opp)
    lax.fori_loop(0, 4, send_opp, 0)

    got_half(opp, 1, opp_r)
    compute(opp, 1, p_opp)
    lax.fori_loop(4, 8, send_opp, 0)
    give_down(0)
    give_up(0)

    got_half(below, 1, below_r)
    compute(below, 1, p_below)
    give_down(1)
    got_half(above, 1, above_r)
    compute(above, 1, p_above)
    give_up(1)

    lax.fori_loop(0, 4, settle, 0)
    dacc[...] = jnp.zeros_like(dacc)
    lax.fori_loop(0, 8, theirs, 0)
    dsend[...] = dacc[...].astype(BF)
    home.start()
    dacc[...] = jnp.zeros_like(dacc)

    def both_ways(k, _):
        settle(k, 0)
        mine(2 * k - 8, 0)
        mine(2 * k - 7, 0)
        return 0

    lax.fori_loop(4, 6, both_ways, 0)
    lax.fori_loop(6, 8, settle, 0)
    lax.fori_loop(4, 8, mine, 0)
    home.wait()
    dout[...] = (dacc[...] + dfar[...].astype(F32)).astype(BF)

    def sent(ref, rows, sem, i):
        pltpu.make_async_copy(ref.at[pl.ds(0, rows)], ref.at[pl.ds(0, rows)], sem.at[i]).wait()

    def last_left(k, _):
        left(k, opp_s)
        return 0

    lax.fori_loop(0, 8, last_left, 0)
    for cp in fars:
        cp.wait_send()
    for a, b in sides + sides_o:
        a.wait_send()
        b.wait_send()
    sent(near, 6 * BLK, fwd_s, 0)
    sent(near, 6 * BLK, fwd_s, 1)
    sent(near, 2 * BLK, side_s, 0)
    sent(near, 2 * BLK, side_s, 1)
    sent(ret_a, ROWS, ret_s, 0)
    sent(ret_b, ROWS, ret_s, 1)
    sent(back, 31 * MSG, back_s, 0)
    sent(back_o, 31 * MSG, backo_s, 0)


def body(tokens, out_grad, probs, ids, wg, wu, wd):
    hbm = pl.BlockSpec(memory_space=pltpu.HBM)
    vm = pl.BlockSpec(memory_space=pltpu.VMEM)
    sd = jax.ShapeDtypeStruct
    wide, slim = sd((ROWS, 2048), BF), sd((ROWS, 1024), BF)
    dma = pltpu.SemaphoreType.DMA
    outs = pl.pallas_call(
        kernel,
        name="expert_backward",
        out_shape=[
            pltpu.VMEM((128, 2048), BF), pltpu.VMEM((2, 2048, 512), F32), pltpu.VMEM((2, 256, 2048), F32),
            wide, wide, wide, wide, slim, slim, slim, slim,
        ],
        in_specs=[hbm, hbm, vm, vm, hbm, hbm, hbm],
        out_specs=[vm] * 3 + [hbm] * 8,
        scratch_shapes=[
            pltpu.VMEM((4, 256, 2048), BF), pltpu.VMEM((4, 256, 2048), BF), pltpu.VMEM((4, 8, 128), F32), pltpu.VMEM((4, 8, 128), F32),
            pltpu.VMEM((ROWS, 2048), BF), pltpu.VMEM((BLK, BLK), BF),
            pltpu.VMEM((HALF, 2048), BF), pltpu.VMEM((2, BLK, 2048), BF), pltpu.VMEM((2, BLK, 2048), BF),
            pltpu.VMEM((BLK, 256), BF), pltpu.VMEM((BLK, 512), BF), pltpu.VMEM((2, BLK, 2048), BF),
            pltpu.VMEM((ROWS, 1024), BF), pltpu.VMEM((ROWS, 1024), BF), pltpu.VMEM((ROWS, 1024), BF), pltpu.VMEM((ROWS, 1024), BF),
            pltpu.VMEM((2 * BLK, 1024), BF), pltpu.VMEM((128, 2048), F32), pltpu.VMEM((128, 2048), BF), pltpu.VMEM((128, 2048), BF),
            pltpu.VMEM((2, 2048, 512), BF), pltpu.VMEM((2, 256, 2048), BF),
            dma((2,)), dma((2,)), dma((5,)), *[dma((4,))] * 8, dma((8,)), dma((8,)), dma((8,)), dma((8,)), dma((2,)), dma((8,)), dma((8,)),
            dma((1,)), dma((2,)), dma((8,)), dma((8,)), dma((1,)), dma((8,)), dma((1,)), dma((8,)), dma((1,)), dma((1,)),
            dma((3,)), dma((4,)), dma((2,)),
        ],
        compiler_params=pltpu.CompilerParams(collective_id=0, has_side_effects=True, vmem_limit_bytes=46 * 2**20),
    )(tokens, out_grad, ids.T, probs.T, wg, wu, wd)
    d, gu, gd = outs[:3]
    return d, gu[:, :, :256], gu[:, :, 256:], gd


def solution(mesh):
    tok = P(("dp", "expert"), None)
    col, row = P("expert", None, "dp"), P("expert", "dp", None)
    return jax.shard_map(
        body, mesh=mesh, in_specs=(tok, tok, tok, tok, col, col, row), out_specs=(tok, col, col, row), check_vma=False
    )
```
